32 devices in a mesh: chain: 2 (over y), px: 8 (over z, x), py: 2 (over core).
Axes of the slice: x: 2, y: 2, z: 4, core: 2. Of those that a mesh axis runs over, the one named last changes fastest.
Arguments:
- adjoint: float32 [512, 256, 256], P(('chain', 'px'), 'py'), parts along dimension 0, may hold values from -6 to 6
- saved: float32 [512, 256, 256], P(('chain', 'px'), 'py'), parts along dimension 0, may hold values from -6 to 6
- spectra: bfloat16 [2, 256, 256, 256], P(None, None, 'px'), may hold values from -6 to 6, as said below
- freq_index: int32 [8], replicated, may hold values from 1 to 8
- picked: int32 [2], replicated, may hold values from 0 to 7
Outputs:
- force: float32 [512, 256, 256], P(('chain', 'px'), 'py'), parts along dimension 0
The draws below stay inside these ranges and needn't reach their ends.
There are 2 independent parts, one for each index of `chain`. The reference program is written for one: setup_inputs(seed, part) draws one part's arguments, and reference() takes and returns one part's arrays. A program takes and returns all parts, laid end to end along the dimension named above; an argument that names none is the same for every part. Nothing has to cross between parts.
Inputs may be any that keep to these rules, and one draw needn't show every extreme that they name: Each kernel is even in every momentum coordinate separately: spectra[j][k1, k2, k3] is unchanged when k1 is replaced by (256 - k1) mod 256, and likewise k2 with 256 and k3 with 256.
All inputs are finite; a program needn't handle non-finite values.
Results may differ from the reference program's by a relative error of at most 0.0003.
Values sent between devices are 32-bit elements; how exact they have to be, the bound alone decides.
No kernel may reach another device: no remote copies, remote signals or barrier semaphores. Data moves between devices by JAX's collectives and lax.ppermute only.
A program may use at most 128 MiB of HBM per device.

```python
import math
import jax
import jax.numpy as jnp

L1 = 256
L2 = 256
L3 = 256
FEATS = 8
WINDOW = 2


def folded_index(length):
    counter = jnp.arange(length, dtype=jnp.int32)
    return jnp.minimum(counter, length - counter).astype(jnp.int32)


def draw_spectra(key, part):
    reduced = jax.random.normal(key, (WINDOW, L1 // 2 + 1, L2 // 2 + 1, L3 // 2 + 1), jnp.float32)
    reduced = jnp.clip(reduced, -6.0, 6.0)
    expanded = jnp.take(reduced, folded_index(L1), axis=1)
    expanded = jnp.take(expanded, folded_index(L2), axis=2)
    expanded = jnp.take(expanded, folded_index(L3), axis=3)
    return expanded.astype(jnp.bfloat16)


def set_ends(drawn, own_key, low, largest):
    extent = drawn.shape
    index_at = [jax.random.randint(jax.random.fold_in(own_key, axis), (), 0, extent[axis]) for axis in range(len(extent))]
    drawn = drawn.at[tuple(index_at)].set(low)
    longest = extent.index(max(extent))
    index_at[longest] = (index_at[longest] + 1) % extent[longest]
    return drawn.at[tuple(index_at)].set(largest)


def levels(key, shape, shards, smallest, largest):
    factor_of = 1.0
    for position, parts in shards:
        heights = jax.random.uniform(jax.random.fold_in(jax.random.fold_in(key, 6), position), (parts,), jnp.float32, smallest / len(shards), largest / len(shards))
        factor_of = factor_of * jnp.repeat(jnp.exp(heights), shape[position] // parts).reshape((-1,) + (1,) * (len(shape) - 1 - position))
    return factor_of


def scatter_about(rng, dims, scale, reach, shards=(), held_as=jnp.bfloat16):
    gain = levels(rng, dims, shards, -0.22, 0.18) if shards else 1.0
    values = jax.random.normal(rng, dims, jnp.float32) * scale * gain
    return jnp.minimum(jnp.maximum(values, -reach), reach).astype(held_as)


def setup_inputs(seed: int = 0, part: int = 0) -> dict:
    arg_keys = jax.random.split(jax.random.key(seed), 6)
    part_splits = jax.random.split(jax.random.fold_in(arg_keys[5], part), 6)
    return {
        "adjoint": scatter_about(part_splits[0], (L1, L2, L3), 1.0, 6.0, ((0, 8), (1, 2)), jnp.float32),
        "saved": scatter_about(part_splits[1], (L1, L2, L3), 1.0, 6.0, ((0, 8), (1, 2)), jnp.float32),
        "spectra": draw_spectra(jax.random.fold_in(arg_keys[5], 71), part),
        "freq_index": set_ends(jax.random.randint(arg_keys[3], (FEATS,), 1, 9), jax.random.fold_in(arg_keys[3], 1), 1, 8).astype(jnp.int32),
        "picked": jax.random.randint(arg_keys[4], (WINDOW,), 0, FEATS).astype(jnp.int32),
    }


def reference(adjoint, saved, spectra, freq_index, picked):
    spectrum = jnp.fft.fftn(adjoint)
    total = jnp.zeros(adjoint.shape, jnp.float32)
    for slot in range(WINDOW):
        omega = (math.pi / 8.0) * freq_index[picked[slot]].astype(jnp.float32)
        field = jnp.real(jnp.fft.ifftn(spectra[slot].astype(jnp.float32) * spectrum))
        total = total + omega * jnp.cos(omega * saved) * field
    return total
```

```python
import math

import jax
import jax.numpy as jnp
import numpy as np
from jax import lax
from jax.experimental import pallas as pl
from jax.experimental.pallas import tpu as pltpu
from jax.sharding import PartitionSpec as P

VMEM_BYTES = 56 * 1024 * 1024
CHUNKS = 2


def hartley(length):
    counter = np.arange(length)
    angle = 2.0 * np.pi * ((counter[:, None] * counter[None, :]) % length) / length
    return np.cos(angle) + np.sin(angle)


def split_table(table):
    high = table.astype(np.float32).astype(jnp.bfloat16)
    low = (table - high.astype(np.float64)).astype(np.float32).astype(jnp.bfloat16)
    return high, low


def left_table(table):
    high, low = split_table(table)
    return np.concatenate([high, high, low], axis=1)


def right_table(table):
    high, low = split_table(table)
    return np.concatenate([high, high, low], axis=0)


def folded_order(length, base):
    half = length // 2
    first = (base + np.arange(half)) % length
    second = (base - np.arange(half)) % length
    second[0] = (base + half) % length
    return np.concatenate([first, second])


def paired_order(length):
    half = length // 2
    order = [0, half]
    for index in range(1, half):
        order += [index, length - index]
    return np.array(order)


def split_value(value):
    high = value.astype(jnp.bfloat16)
    low = (value - high.astype(jnp.float32)).astype(jnp.bfloat16)
    return high, low


def left_dot(table, value):
    high, low = split_value(value)
    stacked = jnp.concatenate([high, low, high], axis=0)
    return jnp.dot(table, stacked, preferred_element_type=jnp.float32)


def right_dot(value, table):
    high, low = split_value(value)
    stacked = jnp.concatenate([high, low, high], axis=1)
    return jnp.dot(stacked, table, preferred_element_type=jnp.float32)


def params():
    return pltpu.CompilerParams(vmem_limit_bytes=VMEM_BYTES)


def forward_last(adjoint, table):
    rows_one, rows_two, length = adjoint.shape
    count = table.shape[0]
    block = min(8, rows_one)

    def body(adjoint_ref, table_ref, out_ref):
        flat = out_ref.reshape(count * block, rows_two)
        for start in range(0, block, 2):
            value = adjoint_ref[start : start + 2].reshape(2 * rows_two, length)
            high, low = split_value(value)
            stacked = jnp.concatenate([high, low, high], axis=1)
            result = lax.dot_general(
                table_ref[...],
                stacked,
                (((1,), (1,)), ((), ())),
                preferred_element_type=jnp.float32,
            )
            for inner in range(2):
                flat[pl.ds(start + inner, count, stride=block), :] = result[
                    :, inner * rows_two : (inner + 1) * rows_two
                ]

    return pl.pallas_call(
        body,
        grid=(rows_one // block,),
        in_specs=[
            pl.BlockSpec((block, rows_two, length), lambda i: (i, 0, 0)),
            pl.BlockSpec(table.shape, lambda i: (0, 0)),
        ],
        out_specs=pl.BlockSpec((count, block, rows_two), lambda i: (0, i, 0)),
        out_shape=jax.ShapeDtypeStruct((count, rows_one, rows_two), jnp.float32),
        compiler_params=params(),
        cost_estimate=pl.CostEstimate(
            flops=6 * count * rows_one * rows_two * length,
            bytes_accessed=4 * rows_one * rows_two * (length + count),
            transcendentals=0,
        ),
        name="forward_last",
    )(adjoint, table)


def filter_planes(planes, kernels, tables):
    width_px, width_py, planes_count, rows_one, rows_two = planes.shape
    slots = kernels.shape[0]
    length_one = width_px * rows_one
    length_two = width_py * rows_two

    def body(planes_ref, kernels_ref, one_f, two_f, one_b, two_b, out_ref):
        value = jnp.concatenate(
            [
                planes_ref[:, part, 0].reshape(length_one, rows_two)
                for part in range(width_py)
            ],
            axis=1,
        )
        value = right_dot(value, two_f[...])
        value = left_dot(one_f[...], value)
        for slot in range(slots):
            product = value * kernels_ref[slot, 0]
            back = left_dot(one_b[...], product)
            back = right_dot(back, two_b[...])
            for part in range(width_py):
                out_ref[:, part, slot, 0] = back[
                    :, part * rows_two : (part + 1) * rows_two
                ].reshape(width_px, rows_one, rows_two)

    plane_size = length_one * length_two
    return pl.pallas_call(
        body,
        grid=(planes_count,),
        in_specs=[
            pl.BlockSpec(
                (width_px, width_py, 1, rows_one, rows_two), lambda i: (0, 0, i, 0, 0)
            ),
            pl.BlockSpec((slots, 1, length_one, length_two), lambda i: (0, i, 0, 0)),
        ]
        + [pl.BlockSpec(table.shape, lambda i: (0, 0)) for table in tables],
        out_specs=pl.BlockSpec(
            (width_px, width_py, slots, 1, rows_one, rows_two),
            lambda i: (0, 0, 0, i, 0, 0),
        ),
        out_shape=jax.ShapeDtypeStruct(
            (width_px, width_py, slots, planes_count, rows_one, rows_two), jnp.float32
        ),
        compiler_params=params(),
        cost_estimate=pl.CostEstimate(
            flops=6 * planes_count * plane_size * (1 + slots) * (length_one + length_two),
            bytes_accessed=planes_count * plane_size * (4 + 6 * slots),
            transcendentals=0,
        ),
        name="filter_planes",
    )(planes, kernels, *tables)


def backward_last(parts, factors, table, total):
    sources, slots, depth, rows_one, rows_two = parts.shape
    length = table.shape[1]
    block = min(8, rows_one)

    def body(*refs):
        if total is None:
            parts_ref, factors_ref, table_ref, out_ref = refs
        else:
            parts_ref, factors_ref, table_ref, total_ref, out_ref = refs
        flat = parts_ref.reshape(sources * slots * depth * block, rows_two)
        for start in range(0, block, 2):
            result = None
            for slot in range(slots):
                values = []
                for inner in range(2):
                    columns = jnp.concatenate(
                        [
                            flat[
                                pl.ds(
                                    (source * slots + slot) * depth * block
                                    + start
                                    + inner,
                                    depth,
                                    stride=block,
                                ),
                                :,
                            ]
                            for source in range(sources)
                        ],
                        axis=0,
                    )
                    values.append(columns.T)
                field = right_dot(jnp.concatenate(values, axis=0), table_ref[...])
                field = field.reshape(2, rows_two, length)
                term = field * factors_ref[slot, start : start + 2]
                result = term if result is None else result + term
            if total is not None:
                result = result + total_ref[start : start + 2]
            out_ref[start : start + 2] = result

    space = pl.BlockSpec((block, rows_two, length), lambda i: (i, 0, 0))
    operands = [parts, factors, table]
    in_specs = [
        pl.BlockSpec(
            (sources, slots, depth, block, rows_two), lambda i: (0, 0, 0, i, 0)
        ),
        pl.BlockSpec((slots, block, rows_two, length), lambda i: (0, i, 0, 0)),
        pl.BlockSpec(table.shape, lambda i: (0, 0)),
    ]
    if total is not None:
        operands.append(total)
        in_specs.append(space)
    size = rows_one * rows_two
    return pl.pallas_call(
        body,
        grid=(rows_one // block,),
        in_specs=in_specs,
        out_specs=space,
        out_shape=jax.ShapeDtypeStruct((rows_one, rows_two, length), jnp.float32),
        compiler_params=params(),
        cost_estimate=pl.CostEstimate(
            flops=6 * slots * size * sources * depth * length,
            bytes_accessed=4 * size * (slots * sources * depth + (2 + slots) * length),
            transcendentals=0,
        ),
        name="backward_last",
    )(*operands)


def cosine_turns():
    points = np.cos(np.pi * (np.arange(64) + 0.5) / 64) * 0.125 + 0.125
    fit = np.polynomial.Polynomial.fit(
        points, np.cos(2.0 * np.pi * np.sqrt(points)), 8, domain=[0.0, 0.25]
    )
    return [float(value) for value in fit.convert().coef]


def cosine_factors(saved, chosen, scale):
    rows_one, rows_two, length = saved.shape
    slots = chosen.shape[0]
    block = min(8, rows_one)
    coefficients = cosine_turns()

    def body(chosen_ref, saved_ref, out_ref):
        for slot in range(slots):
            feature = chosen_ref[slot]
            turns = saved_ref[...] * (feature * (1.0 / 16.0))
            turns = turns - jnp.round(turns)
            square = turns * turns
            result = jnp.full_like(square, coefficients[-1])
            for value in coefficients[-2::-1]:
                result = result * square + value
            out_ref[slot] = result * (feature * (math.pi / 8.0 * scale))

    size = rows_one * rows_two * length
    return pl.pallas_call(
        body,
        grid=(rows_one // block,),
        in_specs=[
            pl.BlockSpec(memory_space=pltpu.SMEM),
            pl.BlockSpec((block, rows_two, length), lambda i: (i, 0, 0)),
        ],
        out_specs=pl.BlockSpec((slots, block, rows_two, length), lambda i: (0, i, 0, 0)),
        out_shape=jax.ShapeDtypeStruct((slots, rows_one, rows_two, length), jnp.float32),
        compiler_params=params(),
        cost_estimate=pl.CostEstimate(
            flops=24 * slots * size, bytes_accessed=4 * size * (1 + slots), transcendentals=0
        ),
        name="cosine_factors",
    )(chosen, saved)


def kernel_planes(spectra, order, width_px, width_py):
    slots, length_one, local_two, length_three = spectra.shape
    half_one = length_one // 2
    half_px = width_px // 2
    devices = width_px * width_py
    own = length_three // devices
    px_index = lax.axis_index("px")
    py_index = lax.axis_index("py")
    folded = np.minimum(order, length_three - order).reshape(devices, own)
    distinct = [list(dict.fromkeys(row.tolist())) for row in folded]
    wanted = max(len(row) for row in distinct)
    padded = np.array([row + [row[-1]] * (wanted - len(row)) for row in distinct])
    place = np.array([[row.index(k) for k in ks] for row, ks in zip(distinct, folded)])
    padded = padded.reshape(2, half_px, width_py, wanted).transpose(0, 2, 1, 3)
    upper = px_index // half_px
    rows = jnp.asarray(padded.reshape(2 * width_py, half_px * wanted))[
        upper * width_py + py_index
    ]
    select = (rows[:, None] == jnp.arange(length_three)[None, :]).astype(jnp.bfloat16)
    pairs = [(0, half_px), (half_px, 0)]
    edge = lax.ppermute(spectra[:, : half_one + 1, 0].astype(jnp.float32), "px", pairs)
    chosen = jnp.einsum(
        "rk,jabk->rjba",
        select,
        spectra[:, : half_one + 1],
        preferred_element_type=jnp.float32,
    )
    chosen_edge = jnp.einsum(
        "rk,jak->rja",
        select.astype(jnp.float32),
        edge,
        precision=lax.Precision.HIGHEST,
        preferred_element_type=jnp.float32,
    )
    chosen = jnp.concatenate([chosen, chosen_edge[:, :, None]], axis=2)
    body = chosen[:, :, :, :half_one]
    last = chosen[:, :, None, :, half_one]
    last = jnp.pad(last, ((0, 0), (0, 0), (0, 0), (0, half_one - local_two - 1)))
    message = jnp.concatenate([body, last], axis=2)
    message = message.reshape(half_px, -1, half_one)
    groups = [list(range(half_px)), list(range(half_px, width_px))]
    message = lax.all_to_all(
        message, "px", 0, 0, axis_index_groups=groups, tiled=True
    )
    message = message.reshape(half_px, wanted, slots, local_two + 2, half_one)
    inner = message[:, :, :, :local_two].transpose(1, 2, 0, 3, 4)
    inner = inner.reshape(wanted, slots, half_px * local_two, half_one)
    edge_two = message[0, :, :, local_two]
    edge_one = message[:, :, :, local_two + 1, :local_two].transpose(1, 2, 0, 3)
    edge_one = edge_one.reshape(wanted, slots, half_px * local_two)
    corner = message[0, :, :, local_two + 1, local_two]
    inner = jnp.swapaxes(inner, 2, 3)
    lower = jnp.concatenate([edge_one[:, :, None], inner[:, :, 1:]], axis=2)
    left = jnp.concatenate([inner, lower], axis=2)
    column = jnp.concatenate([edge_two, corner[..., None], edge_two[..., 1:]], axis=2)
    right = jnp.concatenate([column[..., None], left[..., 1:]], axis=3)
    planes = jnp.concatenate([left, right], axis=3)
    places = jnp.asarray(place)[px_index * width_py + py_index]
    return jnp.take(planes, places, axis=0).transpose(1, 0, 2, 3)


def on_device(adjoint, saved, spectra, freq_index, picked):
    width_px = lax.axis_size("px")
    width_py = lax.axis_size("py")
    devices = width_px * width_py
    rows_one, rows_two, length_three = adjoint.shape
    length_one = rows_one * width_px
    length_two = rows_two * width_py
    slots = picked.shape[0]
    own = length_three // devices
    chunks = CHUNKS if own % (8 * CHUNKS) == 0 else 1
    depth = own // chunks
    order = paired_order(length_three)
    last = hartley(length_three)[order].reshape(devices, chunks, depth, length_three)
    order_one = folded_order(length_one, 0)
    one = hartley(length_one)[order_one]
    one_f = left_table(one)
    one_b = left_table(one.T)
    two = [hartley(length_two)[folded_order(length_two, b)] for b in (0, length_two // 2)]
    upper = lax.axis_index("px") >= width_px // 2
    two_f = jnp.where(upper, right_table(two[1].T), right_table(two[0].T))
    two_b = jnp.where(upper, right_table(two[1]), right_table(two[0]))
    tables = (jnp.asarray(one_f), two_f, jnp.asarray(one_b), two_b)

    feature_ids = jnp.arange(freq_index.shape[0], dtype=jnp.int32)
    chosen = jnp.sum(
        jnp.where(feature_ids[None, :] == picked[:, None], freq_index[None, :], 0), axis=1
    ).astype(jnp.float32)

    arrived = []
    for chunk in range(chunks):
        table = last[:, chunk].reshape(devices * depth, length_three)
        sent = forward_last(adjoint, jnp.asarray(left_table(table)))
        sent = sent.reshape(devices, depth, rows_one, rows_two)
        arrived.append(lax.all_to_all(sent, ("px", "py"), 0, 0, tiled=True))
    planes = kernel_planes(spectra, order, width_px, width_py)
    factors = cosine_factors(saved, chosen, 1.0 / (length_one * length_two * length_three))
    total = None
    returned = []
    for chunk in range(chunks):
        value = arrived[chunk].reshape(width_px, width_py, depth, rows_one, rows_two)
        value = filter_planes(
            value, planes[:, chunk * depth : (chunk + 1) * depth], tables
        )
        value = value.reshape(devices, slots, depth, rows_one, rows_two)
        returned.append(lax.all_to_all(value, ("px", "py"), 0, 0, tiled=True))
    for chunk in range(chunks):
        table = last[:, chunk].reshape(devices * depth, length_three)
        total = backward_last(
            returned[chunk], factors, jnp.asarray(right_table(table)), total
        )
    return total


def solution(mesh):
    placed = (
        P(("chain", "px"), "py", None),
        P(("chain", "px"), "py", None),
        P(None, None, "px", None),
        P(),
        P(),
    )
    return jax.shard_map(
        on_device,
        mesh=mesh,
        in_specs=placed,
        out_specs=P(("chain", "px"), "py", None),
        check_vma=False,
    )
```

```python
import math

import jax
import jax.numpy as jnp
import numpy as np
from jax import lax
from jax.experimental import pallas as pl
from jax.experimental.pallas import tpu as pltpu
from jax.sharding import PartitionSpec as P

VMEM_BYTES = 56 * 1024 * 1024
SHARED = 2


def hartley(length):
    counter = np.arange(length)
    angle = 2.0 * np.pi * ((counter[:, None] * counter[None, :]) % length) / length
    return np.cos(angle) + np.sin(angle)


def split_table(table):
    high = table.astype(np.float32).astype(jnp.bfloat16)
    low = (table - high.astype(np.float64)).astype(np.float32).astype(jnp.bfloat16)
    return high, low


def left_table(table):
    high, low = split_table(table)
    return jnp.asarray(np.concatenate([high, high, low], axis=1))


def right_table(table):
    high, low = split_table(table)
    return jnp.asarray(np.concatenate([high, high, low], axis=0))


def traced_table(rows, columns, length, axis):
    product = rows[:, None] * columns[None, :] % length
    angle = product.astype(jnp.float32) * (2.0 * math.pi / length)
    value = jnp.cos(angle) + jnp.sin(angle)
    high = lax.reduce_precision(value, 8, 7)
    low = value - high
    return jnp.concatenate([high, high, low], axis=axis).astype(jnp.bfloat16)


def partners(first, length):
    base = first % (length // 2) == 0
    return jnp.where(base, (first + length // 2) % length, (length - first) % length)


def paired_order(length):
    half = length // 2
    order = [0, half]
    for index in range(1, half):
        order += [index, length - index]
    return np.array(order)


def split_value(value):
    high = value.astype(jnp.bfloat16)
    low = (value - high.astype(jnp.float32)).astype(jnp.bfloat16)
    return high, low


def left_dot(table, value):
    high, low = split_value(value)
    stacked = jnp.concatenate([high, low, high], axis=0)
    return jnp.dot(table, stacked, preferred_element_type=jnp.float32)


def right_dot(value, table):
    high, low = split_value(value)
    stacked = jnp.concatenate([high, low, high], axis=1)
    return jnp.dot(stacked, table, preferred_element_type=jnp.float32)


def params():
    return pltpu.CompilerParams(vmem_limit_bytes=VMEM_BYTES)


def forward_last(adjoint, table, copies):
    rows_one, rows_two, length = adjoint.shape
    count = table.shape[0]
    block = min(8, rows_one)

    def body(adjoint_ref, table_ref, out_ref):
        flat = out_ref.reshape(copies * count * block, rows_two)
        for start in range(0, block, 2):
            value = adjoint_ref[start : start + 2].reshape(2 * rows_two, length)
            high, low = split_value(value)
            stacked = jnp.concatenate([high, low, high], axis=1)
            result = lax.dot_general(
                table_ref[...],
                stacked,
                (((1,), (1,)), ((), ())),
                preferred_element_type=jnp.float32,
            )
            for inner in range(2):
                piece = result[:, inner * rows_two : (inner + 1) * rows_two]
                for copy in range(copies):
                    first = copy * count * block + start + inner
                    flat[pl.ds(first, count, stride=block), :] = piece

    return pl.pallas_call(
        body,
        grid=(rows_one // block,),
        in_specs=[
            pl.BlockSpec((block, rows_two, length), lambda i: (i, 0, 0)),
            pl.BlockSpec(table.shape, lambda i: (0, 0)),
        ],
        out_specs=pl.BlockSpec((copies, count, block, rows_two), lambda i: (0, 0, i, 0)),
        out_shape=jax.ShapeDtypeStruct((copies, count, rows_one, rows_two), jnp.float32),
        compiler_params=params(),
        cost_estimate=pl.CostEstimate(
            flops=6 * count * rows_one * rows_two * length,
            bytes_accessed=4 * rows_one * rows_two * (length + copies * count),
            transcendentals=0,
        ),
        name="forward_last",
    )(adjoint, table)


def whole_plane(message_refs, slot, slots, special, local_two):
    blocks = [ref[0] for ref in message_refs]
    body = [block[slot * local_two : (slot + 1) * local_two] for block in blocks]
    folded = jnp.concatenate(body, axis=0)
    first = slots * local_two + 3 * slot
    edges = blocks[0][first : first + 3]
    for block in blocks[1:]:
        edges = edges + block[first : first + 3]
    edge_two, edge_one, corner = edges[0:1], edges[1:2], edges[2:3]
    extent = folded.shape
    row = lax.broadcasted_iota(jnp.int32, extent, 0)
    column = lax.broadcasted_iota(jnp.int32, extent, 1)
    right = jnp.where(row == special, edge_two, folded).T
    left = folded.T
    top = row == 0
    lower_left = jnp.where(top, edge_one, left)
    lower_right = jnp.where(top, jnp.where(column == special, corner, edge_one), right)
    return jnp.concatenate(
        [
            jnp.concatenate([left, right], axis=1),
            jnp.concatenate([lower_left, lower_right], axis=1),
        ],
        axis=0,
    )


def filter_planes(planes, messages, places, special, tables, slots, split):
    width_px, width_py, planes_count, rows_one, rows_two = planes.shape
    length_one = width_px * rows_one
    length_two = width_py * rows_two
    out_px = tables[2].shape[0] // rows_one
    message_rows = messages[0].shape[1]
    local_two = length_two // 2 // len(messages)

    def body(places_ref, special_ref, planes_ref, *refs):
        message_refs = refs[: len(messages)]
        one_f, two_f, one_b, two_b = refs[len(messages) : len(messages) + 4]
        out_refs = refs[len(messages) + 4 :]
        value = jnp.concatenate(
            [
                planes_ref[:, part, 0].reshape(length_one, rows_two)
                for part in range(width_py)
            ],
            axis=1,
        )
        value = right_dot(value, two_f[...])
        value = left_dot(one_f[...], value)
        for slot in range(slots):
            plane = whole_plane(message_refs, slot, slots, special_ref[0], local_two)
            back = left_dot(one_b[...], value * plane)
            back = right_dot(back, two_b[...])
            for part in range(width_py):
                piece = back[:, part * rows_two : (part + 1) * rows_two]
                if split:
                    for index in range(out_px):
                        out_refs[index][part, slot, 0] = piece[
                            index * rows_one : (index + 1) * rows_one
                        ]
                else:
                    out_refs[0][:, part, slot, 0] = piece.reshape(
                        out_px, rows_one, rows_two
                    )

    plane_size = length_one * length_two
    if split:
        extent = (width_py, slots, planes_count, rows_one, rows_two)
        out_shape = [jax.ShapeDtypeStruct(extent, jnp.float32)] * out_px
        out_specs = [
            pl.BlockSpec(
                (width_py, slots, 1, rows_one, rows_two), lambda i, *_: (0, 0, i, 0, 0)
            )
        ] * out_px
    else:
        extent = (out_px, width_py, slots, planes_count, rows_one, rows_two)
        out_shape = [jax.ShapeDtypeStruct(extent, jnp.float32)]
        out_specs = [
            pl.BlockSpec(
                (out_px, width_py, slots, 1, rows_one, rows_two),
                lambda i, *_: (0, 0, 0, i, 0, 0),
            )
        ]
    out_rows = out_px * rows_one
    outs = pl.pallas_call(
        body,
        grid_spec=pltpu.PrefetchScalarGridSpec(
            num_scalar_prefetch=2,
            grid=(planes_count,),
            in_specs=[
                pl.BlockSpec(
                    (width_px, width_py, 1, rows_one, rows_two),
                    lambda i, *_: (0, 0, i, 0, 0),
                )
            ]
            + [
                pl.BlockSpec(
                    (1, message_rows, length_one // 2),
                    lambda i, places_ref, special_ref: (places_ref[i], 0, 0),
                )
            ]
            * len(messages)
            + [pl.BlockSpec(table.shape, lambda i, *_: (0, 0)) for table in tables],
            out_specs=out_specs,
        ),
        out_shape=out_shape,
        compiler_params=params(),
        cost_estimate=pl.CostEstimate(
            flops=6
            * planes_count
            * (
                plane_size * (length_one + length_two)
                + slots * out_rows * length_two * (length_one + length_two)
            ),
            bytes_accessed=4
            * planes_count
            * (plane_size + slots * (plane_size // 4 + out_rows * length_two)),
            transcendentals=0,
        ),
        name="filter_planes",
    )(places, special, planes, *messages, *tables)
    return outs if split else outs[0]


def backward_last(groups, factors, total):
    parts = [part for members, _ in groups for part in members]
    tables = [table for _, table in groups]
    slots = factors.shape[0]
    rows_one, rows_two = parts[0].shape[3:]
    length = tables[0].shape[1]
    block = min(8, rows_one)

    def body(*refs):
        factors_ref = refs[0]
        table_refs = refs[1 : 1 + len(groups)]
        part_refs = refs[1 + len(groups) : 1 + len(groups) + len(parts)]
        out_ref = refs[-1]
        flats = [
            ref.reshape(math.prod(part.shape[:3]) * block, rows_two)
            for ref, part in zip(part_refs, parts)
        ]

        def columns(slot, site, first, last):
            found = []
            for index in range(first, last):
                sources, _, depth = parts[index].shape[:3]
                for source in range(sources):
                    row = (source * slots + slot) * depth * block + site
                    found.append(flats[index][pl.ds(row, depth, stride=block), :])
            return jnp.concatenate(found, axis=0).T

        for start in range(0, block, 2):
            result = None
            for slot in range(slots):
                field = None
                first = 0
                for (members, _), table_ref in zip(groups, table_refs):
                    last = first + len(members)
                    value = jnp.concatenate(
                        [columns(slot, start + inner, first, last) for inner in range(2)],
                        axis=0,
                    )
                    value = right_dot(value, table_ref[...])
                    field = value if field is None else field + value
                    first = last
                field = field.reshape(2, rows_two, length)
                term = field * factors_ref[slot, start : start + 2]
                result = term if result is None else result + term
            if total is not None:
                result = result + refs[-2][start : start + 2]
            out_ref[start : start + 2] = result

    space = pl.BlockSpec((block, rows_two, length), lambda i: (i, 0, 0))
    operands = [factors] + tables + parts
    in_specs = (
        [pl.BlockSpec((slots, block, rows_two, length), lambda i: (0, i, 0, 0))]
        + [pl.BlockSpec(table.shape, lambda i: (0, 0)) for table in tables]
        + [
            pl.BlockSpec(part.shape[:3] + (block, rows_two), lambda i: (0, 0, 0, i, 0))
            for part in parts
        ]
    )
    if total is not None:
        operands.append(total)
        in_specs.append(space)
    size = rows_one * rows_two
    planes_count = sum(part.shape[0] * part.shape[2] for part in parts)
    return pl.pallas_call(
        body,
        grid=(rows_one // block,),
        in_specs=in_specs,
        out_specs=space,
        out_shape=jax.ShapeDtypeStruct((rows_one, rows_two, length), jnp.float32),
        compiler_params=params(),
        cost_estimate=pl.CostEstimate(
            flops=6 * slots * size * planes_count * length,
            bytes_accessed=4 * size * (slots * planes_count + (2 + slots) * length),
            transcendentals=0,
        ),
        name="backward_last",
    )(*operands)


def cosine_turns():
    points = np.cos(np.pi * (np.arange(64) + 0.5) / 64) * 0.125 + 0.125
    fit = np.polynomial.Polynomial.fit(
        points, np.cos(2.0 * np.pi * np.sqrt(points)), 8, domain=[0.0, 0.25]
    )
    return [float(value) for value in fit.convert().coef]


def cosine_factors(saved, chosen, scale):
    rows_one, rows_two, length = saved.shape
    slots = chosen.shape[0]
    block = min(8, rows_one)
    coefficients = cosine_turns()

    def body(chosen_ref, saved_ref, out_ref):
        for slot in range(slots):
            feature = chosen_ref[slot]
            turns = saved_ref[...] * (feature * (1.0 / 16.0))
            turns = turns - jnp.round(turns)
            square = turns * turns
            result = jnp.full_like(square, coefficients[-1])
            for value in coefficients[-2::-1]:
                result = result * square + value
            out_ref[slot] = result * (feature * (math.pi / 8.0 * scale))

    size = rows_one * rows_two * length
    return pl.pallas_call(
        body,
        grid=(rows_one // block,),
        in_specs=[
            pl.BlockSpec(memory_space=pltpu.SMEM),
            pl.BlockSpec((block, rows_two, length), lambda i: (i, 0, 0)),
        ],
        out_specs=pl.BlockSpec((slots, block, rows_two, length), lambda i: (0, i, 0, 0)),
        out_shape=jax.ShapeDtypeStruct((slots, rows_one, rows_two, length), jnp.float32),
        compiler_params=params(),
        cost_estimate=pl.CostEstimate(
            flops=24 * slots * size, bytes_accessed=4 * size * (1 + slots), transcendentals=0
        ),
        name="cosine_factors",
    )(chosen, saved)


def swap_pairs(width_px, half_px, delta):
    return [(px, px // half_px * half_px + (px % half_px ^ delta)) for px in range(width_px)]


def send_messages(message, width_px):
    half_px = width_px // 2
    if half_px <= 8:
        return [message[0]] + [
            lax.ppermute(message[delta], "px", swap_pairs(width_px, half_px, delta))
            for delta in range(1, half_px)
        ]
    groups = [list(range(half_px)), list(range(half_px, width_px))]
    index = lax.axis_index("px") % half_px ^ jnp.arange(half_px)
    message = jnp.take(jnp.stack(message), index, axis=0)
    message = lax.all_to_all(message, "px", 0, 0, axis_index_groups=groups, tiled=True)
    message = jnp.take(message, index, axis=0)
    return [message[delta] for delta in range(half_px)]


def message_rows(spectra, edge, select, count):
    slots, length_one, local_two, length_three = spectra.shape
    half_one = length_one // 2
    half_px = half_one // local_two
    padded = select.shape[0] // half_px
    used = slots * (local_two + 3)
    extent = used + -used % 8
    group = 4
    lanes = 128

    def body(spectra_ref, edge_ref, select_ref, *refs):
        flats = [ref.reshape(count * extent, half_one) for ref in refs[:half_px]]
        scratch = refs[half_px:]

        def chosen(value):
            return lax.dot_general(
                select_ref[...],
                value.astype(jnp.bfloat16),
                (((1,), (1,)), ((), ())),
                preferred_element_type=jnp.float32,
            )

        def store(value, row):
            for delta in range(half_px):
                flats[delta][pl.ds(row, count, stride=extent), :] = value[
                    delta * padded : delta * padded + count
                ]

        for slot in range(slots):
            for part, ref in enumerate(scratch):
                ref[...] = (
                    spectra_ref[slot, :half_one, :, part * lanes : (part + 1) * lanes]
                    .astype(jnp.float32)
                    .reshape(half_one * local_two, lanes)
                )
            for start in range(0, local_two, group):
                value = jnp.concatenate(
                    [
                        jnp.concatenate(
                            [
                                ref[pl.ds(start + inner, half_one, stride=local_two), :]
                                for ref in scratch
                            ],
                            axis=1,
                        )
                        for inner in range(group)
                    ],
                    axis=0,
                )
                value = chosen(value)
                for inner in range(group):
                    store(
                        value[:, inner * half_one : (inner + 1) * half_one],
                        slot * local_two + start + inner,
                    )
            first = slots * local_two + 3 * slot
            store(chosen(edge_ref[slot, :half_one]), first)
            tiled = jnp.concatenate([spectra_ref[slot, half_one]] * half_px, axis=0)
            value = chosen(tiled)
            row = lax.broadcasted_iota(jnp.int32, value.shape, 0) // padded
            lane = lax.broadcasted_iota(jnp.int32, value.shape, 1) // local_two
            store(jnp.where(row == lane, value, 0.0), first + 1)
            corner = edge_ref[slot, half_one : half_one + 1]
            store(chosen(jnp.broadcast_to(corner, (half_one, length_three))), first + 2)
        for flat in flats:
            for row in range(used, extent):
                flat[pl.ds(row, count, stride=extent), :] = jnp.zeros(
                    (count, half_one), jnp.float32
                )

    part = (slots, half_one + 1, local_two, length_three)
    return pl.pallas_call(
        body,
        grid=(1,),
        in_specs=[
            pl.BlockSpec(part, lambda i: (0, 0, 0, 0)),
            pl.BlockSpec(edge.shape, lambda i: (0, 0, 0)),
            pl.BlockSpec(select.shape, lambda i: (0, 0)),
        ],
        out_specs=[pl.BlockSpec((count, extent, half_one), lambda i: (0, 0, 0))] * half_px,
        out_shape=[jax.ShapeDtypeStruct((count, extent, half_one), jnp.float32)] * half_px,
        scratch_shapes=[pltpu.VMEM((half_one * local_two, lanes), jnp.float32)]
        * (length_three // lanes),
        compiler_params=params(),
        cost_estimate=pl.CostEstimate(
            flops=2 * slots * select.shape[0] * half_one * local_two * length_three,
            bytes_accessed=2 * math.prod(part) + 4 * half_px * count * extent * half_one,
            transcendentals=0,
        ),
        name="message_rows",
    )(spectra, edge, select)


def kernel_messages(spectra, edge, wanted, width_px, width_py):
    slots, length_one, local_two, length_three = spectra.shape
    half_one = length_one // 2
    half_px = width_px // 2
    count = wanted.shape[1]
    px_index = lax.axis_index("px")
    py_index = lax.axis_index("py")
    wanted = wanted.reshape(width_px, width_py, count)
    sources = np.arange(width_px)
    targets = np.stack(
        [sources // half_px * half_px + (sources % half_px ^ d) for d in range(half_px)],
        axis=1,
    )
    rows = jnp.asarray(wanted[targets].transpose(0, 2, 1, 3).reshape(-1, half_px * count))
    rows = rows[px_index * width_py + py_index]
    sublanes = 16
    if local_two % sublanes == 0:
        padded = count + -count % sublanes
        rows = rows.reshape(half_px, count)
        rows = jnp.pad(rows, ((0, 0), (0, padded - count)), constant_values=-1)
        rows = rows.reshape(-1)
        select = (rows[:, None] == jnp.arange(length_three)[None, :]).astype(jnp.bfloat16)
        return message_rows(spectra, edge, select, count)
    select = (rows[:, None] == jnp.arange(length_three)[None, :]).astype(jnp.bfloat16)
    chosen = jnp.einsum(
        "rk,jabk->rjba",
        select,
        spectra[:, : half_one + 1],
        preferred_element_type=jnp.float32,
    )
    chosen_edge = jnp.einsum(
        "rk,jak->rja",
        select.astype(jnp.float32),
        edge,
        precision=lax.Precision.HIGHEST,
        preferred_element_type=jnp.float32,
    )
    body = chosen[..., :half_one].reshape(half_px, count, slots * local_two, half_one)
    edge_two = chosen_edge[..., None, :half_one]
    corner = jnp.broadcast_to(chosen_edge[..., None, half_one:], edge_two.shape)
    last = chosen[..., half_one].reshape(half_px, count, slots, local_two)
    edge_one = jnp.stack(
        [
            jnp.pad(
                last[delta],
                (
                    (0, 0),
                    (0, 0),
                    (delta * local_two, (half_px - 1 - delta) * local_two),
                ),
            )
            for delta in range(half_px)
        ]
    )
    edge_one = edge_one.reshape(half_px * count, slots, 1, half_px * local_two)
    edges = jnp.concatenate([edge_two, edge_one, corner], axis=2)
    edges = edges.reshape(half_px, count, 3 * slots, half_one)
    spare = -(slots * (local_two + 3)) % 8
    message = jnp.concatenate([body, edges], axis=2)
    message = jnp.pad(message, ((0, 0), (0, 0), (0, spare), (0, 0)))
    return [message[delta] for delta in range(half_px)]


def on_device(adjoint, saved, spectra, freq_index, picked):
    width_px = lax.axis_size("px")
    width_py = lax.axis_size("py")
    px_index = lax.axis_index("px")
    py_index = lax.axis_index("py")
    devices = width_px * width_py
    half_px = width_px // 2
    half_devices = devices // 2
    half_index = px_index // half_px
    px_low = px_index % half_px
    rows_one, rows_two, length_three = adjoint.shape
    length_one = rows_one * width_px
    length_two = rows_two * width_py
    slots = picked.shape[0]

    order = paired_order(length_three)
    shared_depth = 8
    shared_chunks = SHARED if length_three % (8 * devices * SHARED) == 0 else 0
    shared_count = half_devices * shared_depth
    shared = [
        order[chunk * shared_count : (chunk + 1) * shared_count].reshape(half_devices, -1)
        for chunk in range(shared_chunks)
    ]
    single = order[shared_chunks * shared_count :].reshape(devices, -1)
    depth = single.shape[1]
    owned = [np.concatenate([chunk, chunk]) for chunk in shared] + [single]
    folded = np.concatenate(owned, axis=1)
    folded = np.minimum(folded, length_three - folded)
    distinct = [list(dict.fromkeys(row.tolist())) for row in folded]
    count = max(len(row) for row in distinct)
    wanted = np.array([row + [row[-1]] * (count - len(row)) for row in distinct])
    places = np.array([[row.index(k) for k in ks] for row, ks in zip(distinct, folded)])

    half_one = length_one // 2
    edge = lax.ppermute(
        spectra[:, : half_one + 1, 0].astype(jnp.float32),
        "px",
        [(0, half_px), (half_px, 0)],
    )
    last = hartley(length_three)
    sent_shared = []
    for chunk in shared:
        sent_shared.append(
            forward_last(adjoint, left_table(last[chunk.reshape(-1)]), 2).reshape(
                devices, shared_depth, rows_one, rows_two
            )
        )
    sent_single = forward_last(adjoint, left_table(last[single.reshape(-1)]), 1).reshape(
        devices, depth, rows_one, rows_two
    )

    def exchange(value):
        return lax.all_to_all(value, ("px", "py"), 0, 0, tiled=True)

    def arranged(value):
        return value.reshape(width_px, width_py, -1, rows_one, rows_two)

    if shared_chunks:
        sent_shared[0], spectra, edge = lax.optimization_barrier(
            (sent_shared[0], spectra, edge)
        )
    messages = kernel_messages(spectra, edge, wanted, width_px, width_py)
    messages = send_messages(messages, width_px)
    if shared_chunks:
        sent_single, messages = lax.optimization_barrier((sent_single, messages))
    places = jnp.asarray(places, dtype=jnp.int32)[px_index * width_py + py_index]
    local_two = length_two // width_px
    special = (px_low * local_two).astype(jnp.int32).reshape(1)

    order_one = np.arange(length_one // 2)
    order_one = np.concatenate([order_one, (length_one - order_one) % length_one])
    order_one[length_one // 2] = length_one // 2
    slabs = half_index * half_px + (px_low ^ jnp.arange(half_px))
    order_two = (slabs[:, None] * local_two + jnp.arange(local_two)[None, :]).reshape(-1)
    order_two = jnp.concatenate([order_two, partners(order_two, length_two)])
    one = hartley(length_one)[order_one]
    one_f = left_table(one)
    one_b = left_table(one.T)
    sites_two = jnp.arange(length_two)
    two_f = traced_table(sites_two, order_two, length_two, 0)
    two_b = traced_table(order_two, sites_two, length_two, 0)
    sites_half = (slabs[:, None] * rows_one + jnp.arange(rows_one)[None, :]).reshape(-1)
    half_one_b = traced_table(sites_half, jnp.asarray(order_one), length_one, 1)
    near_two = (sites_two + py_index * rows_two) % length_two
    near_two_b = traced_table(order_two, near_two, length_two, 0)
    tables = (one_f, two_f, one_b, two_b)
    half_tables = (one_f, two_f, half_one_b, near_two_b)

    feature_ids = jnp.arange(freq_index.shape[0], dtype=jnp.int32)
    chosen = jnp.sum(
        jnp.where(feature_ids[None, :] == picked[:, None], freq_index[None, :], 0), axis=1
    ).astype(jnp.float32)

    shared_source = (
        (px_low ^ jnp.arange(half_px))[None, :] * width_py
        + ((py_index - jnp.arange(width_py)) % width_py)[:, None]
    ).reshape(-1)

    def shared_fields(index, value):
        first = index * shared_depth
        return filter_planes(
            arranged(value),
            messages,
            places[first : first + shared_depth],
            special,
            half_tables,
            slots,
            True,
        )

    def shared_rows(pieces):
        return [pieces[0]] + [
            lax.ppermute(pieces[delta], "px", swap_pairs(width_px, half_px, delta))
            for delta in range(1, half_px)
        ]

    def shared_group(index, pieces):
        parts = [jnp.stack([piece[0] for piece in pieces])]
        for shift in range(1, width_py):
            pairs = [(c, (c + shift) % width_py) for c in range(width_py)]
            far = jnp.stack([piece[shift] for piece in pieces])
            parts.append(lax.ppermute(far, "py", pairs))
        ids = jnp.asarray(shared[index])[shared_source].reshape(-1)
        return parts, traced_table(ids, jnp.arange(length_three), length_three, 0)

    barrier = lax.optimization_barrier
    factors = cosine_factors(saved, chosen, 1.0 / (length_one * length_two * length_three))
    single_table = right_table(last[single.reshape(-1)])
    first = shared_chunks * shared_depth

    def single_fields(value):
        return filter_planes(
            arranged(value),
            messages,
            places[first : first + depth],
            special,
            tables,
            slots,
            False,
        ).reshape(devices, slots, depth, rows_one, rows_two)

    if shared_chunks == 0:
        returned = exchange(single_fields(exchange(sent_single)))
        return backward_last([([returned], single_table)], factors, None)

    arrived = exchange(sent_shared[0])
    arrived_single = exchange(sent_single)
    pieces = shared_fields(0, arrived)
    pieces, sent_shared[1] = barrier((pieces, sent_shared[1]))
    near = shared_rows(pieces)
    arrived = exchange(sent_shared[1])
    fields_single = single_fields(arrived_single)
    fields_single, factors, near = barrier((fields_single, factors, near))
    returned = exchange(fields_single)
    pieces = shared_fields(1, arrived)
    pieces, near = barrier((pieces, near))
    group = shared_group(0, near)
    late = shared_rows(pieces)
    total = backward_last([group], factors, None)
    late, total = barrier((late, total))
    return backward_last(
        [shared_group(1, late), ([returned], single_table)], factors, total
    )


def solution(mesh):
    placed = (
        P(("chain", "px"), "py", None),
        P(("chain", "px"), "py", None),
        P(None, None, "px", None),
        P(),
        P(),
    )
    return jax.shard_map(
        on_device,
        mesh=mesh,
        in_specs=placed,
        out_specs=P(("chain", "px"), "py", None),
        check_vma=False,
    )
```

```python
import math

import jax
import jax.numpy as jnp
import numpy as np
from jax import lax
from jax.experimental import pallas as pl
from jax.experimental.pallas import tpu as pltpu
from jax.sharding import PartitionSpec as P

VMEM_BYTES = 56 * 1024 * 1024
SHARED = 2


def hartley(length):
    counter = np.arange(length)
    angle = 2.0 * np.pi * ((counter[:, None] * counter[None, :]) % length) / length
    return np.cos(angle) + np.sin(angle)


def split_table(table):
    high = table.astype(np.float32).astype(jnp.bfloat16)
    low = (table - high.astype(np.float64)).astype(np.float32).astype(jnp.bfloat16)
    return high, low


def left_table(table):
    high, low = split_table(table)
    return jnp.asarray(np.concatenate([high, high, low], axis=1))


def right_table(table):
    high, low = split_table(table)
    return jnp.asarray(np.concatenate([high, high, low], axis=0))


def traced_table(rows, columns, length, axis):
    product = rows[:, None] * columns[None, :] % length
    angle = product.astype(jnp.float32) * (2.0 * math.pi / length)
    value = jnp.cos(angle) + jnp.sin(angle)
    high = lax.reduce_precision(value, 8, 7)
    low = value - high
    return jnp.concatenate([high, high, low], axis=axis).astype(jnp.bfloat16)


def partners(first, length):
    base = first % (length // 2) == 0
    return jnp.where(base, (first + length // 2) % length, (length - first) % length)


def paired_order(length):
    half = length // 2
    order = [0, half]
    for index in range(1, half):
        order += [index, length - index]
    return np.array(order)


def split_value(value):
    high = value.astype(jnp.bfloat16)
    low = (value - high.astype(jnp.float32)).astype(jnp.bfloat16)
    return high, low


def left_dot(table, value):
    high, low = split_value(value)
    stacked = jnp.concatenate([high, low, high], axis=0)
    return jnp.dot(table, stacked, preferred_element_type=jnp.float32)


def right_dot(value, table):
    high, low = split_value(value)
    stacked = jnp.concatenate([high, low, high], axis=1)
    return jnp.dot(stacked, table, preferred_element_type=jnp.float32)


def params():
    return pltpu.CompilerParams(vmem_limit_bytes=VMEM_BYTES)


def forward_last(adjoint, table, depth, copies):
    rows_one, rows_two, length = adjoint.shape
    count = table.shape[0]
    block = min(8, rows_one)

    def body(adjoint_ref, table_ref, out_ref):
        flat = out_ref.reshape(depth * block, rows_two)
        for start in range(0, block, 2):
            value = adjoint_ref[start : start + 2].reshape(2 * rows_two, length)
            high, low = split_value(value)
            stacked = jnp.concatenate([high, low, high], axis=1)
            result = lax.dot_general(
                table_ref[...],
                stacked,
                (((1,), (1,)), ((), ())),
                preferred_element_type=jnp.float32,
            )
            for inner in range(2):
                columns = slice(inner * rows_two, (inner + 1) * rows_two)
                for row, rows, planes in copies:
                    for plane in planes:
                        flat[
                            pl.ds(plane * block + start + inner, rows, stride=block), :
                        ] = result[row : row + rows, columns]

    return pl.pallas_call(
        body,
        grid=(rows_one // block,),
        in_specs=[
            pl.BlockSpec((block, rows_two, length), lambda i: (i, 0, 0)),
            pl.BlockSpec(table.shape, lambda i: (0, 0)),
        ],
        out_specs=pl.BlockSpec((depth, block, rows_two), lambda i: (0, i, 0)),
        out_shape=jax.ShapeDtypeStruct((depth, rows_one, rows_two), jnp.float32),
        compiler_params=params(),
        cost_estimate=pl.CostEstimate(
            flops=6 * count * rows_one * rows_two * length,
            bytes_accessed=4 * rows_one * rows_two * (length + depth),
            transcendentals=0,
        ),
        name="forward_last",
    )(adjoint, table)


def whole_plane(message_refs, slot, slots, special, local_two):
    blocks = [ref[0] for ref in message_refs]
    body = [block[slot * local_two : (slot + 1) * local_two] for block in blocks]
    folded = jnp.concatenate(body, axis=0)
    first = slots * local_two + 3 * slot
    edges = blocks[0][first : first + 3]
    for block in blocks[1:]:
        edges = edges + block[first : first + 3]
    edge_two, edge_one, corner = edges[0:1], edges[1:2], edges[2:3]
    extent = folded.shape
    row = lax.broadcasted_iota(jnp.int32, extent, 0)
    column = lax.broadcasted_iota(jnp.int32, extent, 1)
    right = jnp.where(row == special, edge_two, folded).T
    left = folded.T
    top = row == 0
    lower_left = jnp.where(top, edge_one, left)
    lower_right = jnp.where(top, jnp.where(column == special, corner, edge_one), right)
    return jnp.concatenate(
        [
            jnp.concatenate([left, right], axis=1),
            jnp.concatenate([lower_left, lower_right], axis=1),
        ],
        axis=0,
    )


def filter_planes(planes, first, messages, places, special, tables, slots, split):
    width_px, width_py, _, rows_one, rows_two = planes.shape
    planes_count = places.shape[0]
    length_one = width_px * rows_one
    length_two = width_py * rows_two
    out_px = tables[2].shape[0] // rows_one
    message_rows = messages[0].shape[1]
    local_two = length_two // 2 // len(messages)

    def body(places_ref, special_ref, planes_ref, *refs):
        message_refs = refs[: len(messages)]
        one_f, two_f, one_b, two_b = refs[len(messages) : len(messages) + 4]
        out_refs = refs[len(messages) + 4 :]
        value = jnp.concatenate(
            [
                planes_ref[:, part, 0].reshape(length_one, rows_two)
                for part in range(width_py)
            ],
            axis=1,
        )
        value = right_dot(value, two_f[...])
        value = left_dot(one_f[...], value)
        for slot in range(slots):
            plane = whole_plane(message_refs, slot, slots, special_ref[0], local_two)
            back = left_dot(one_b[...], value * plane)
            back = right_dot(back, two_b[...])
            for part in range(width_py):
                piece = back[:, part * rows_two : (part + 1) * rows_two]
                if split:
                    for index in range(out_px):
                        out_refs[index][part, slot, 0] = piece[
                            index * rows_one : (index + 1) * rows_one
                        ]
                else:
                    out_refs[0][:, part, slot, 0] = piece.reshape(
                        out_px, rows_one, rows_two
                    )

    plane_size = length_one * length_two
    if split:
        extent = (width_py, slots, planes_count, rows_one, rows_two)
        out_shape = [jax.ShapeDtypeStruct(extent, jnp.float32)] * out_px
        out_specs = [
            pl.BlockSpec(
                (width_py, slots, 1, rows_one, rows_two), lambda i, *_: (0, 0, i, 0, 0)
            )
        ] * out_px
    else:
        extent = (out_px, width_py, slots, planes_count, rows_one, rows_two)
        out_shape = [jax.ShapeDtypeStruct(extent, jnp.float32)]
        out_specs = [
            pl.BlockSpec(
                (out_px, width_py, slots, 1, rows_one, rows_two),
                lambda i, *_: (0, 0, 0, i, 0, 0),
            )
        ]
    out_rows = out_px * rows_one
    outs = pl.pallas_call(
        body,
        grid_spec=pltpu.PrefetchScalarGridSpec(
            num_scalar_prefetch=2,
            grid=(planes_count,),
            in_specs=[
                pl.BlockSpec(
                    (width_px, width_py, 1, rows_one, rows_two),
                    lambda i, *_: (0, 0, first + i, 0, 0),
                )
            ]
            + [
                pl.BlockSpec(
                    (1, message_rows, length_one // 2),
                    lambda i, places_ref, special_ref: (places_ref[i], 0, 0),
                )
            ]
            * len(messages)
            + [pl.BlockSpec(table.shape, lambda i, *_: (0, 0)) for table in tables],
            out_specs=out_specs,
        ),
        out_shape=out_shape,
        compiler_params=params(),
        cost_estimate=pl.CostEstimate(
            flops=6
            * planes_count
            * (
                plane_size * (length_one + length_two)
                + slots * out_rows * length_two * (length_one + length_two)
            ),
            bytes_accessed=4
            * planes_count
            * (plane_size + slots * (plane_size // 4 + out_rows * length_two)),
            transcendentals=0,
        ),
        name="filter_planes",
    )(places, special, planes, *messages, *tables)
    return outs if split else outs[0]


def backward_last(groups, factors, total):
    parts = [part for members, _ in groups for part in members]
    tables = [table for _, table in groups]
    slots = factors.shape[0]
    rows_one, rows_two = parts[0].shape[3:]
    length = tables[0].shape[1]
    block = min(8, rows_one)

    def body(*refs):
        factors_ref = refs[0]
        table_refs = refs[1 : 1 + len(groups)]
        part_refs = refs[1 + len(groups) : 1 + len(groups) + len(parts)]
        out_ref = refs[-1]
        flats = [
            ref.reshape(math.prod(part.shape[:3]) * block, rows_two)
            for ref, part in zip(part_refs, parts)
        ]

        def columns(slot, site, first, last):
            found = []
            for index in range(first, last):
                sources, _, depth = parts[index].shape[:3]
                for source in range(sources):
                    row = (source * slots + slot) * depth * block + site
                    found.append(flats[index][pl.ds(row, depth, stride=block), :])
            return jnp.concatenate(found, axis=0).T

        for start in range(0, block, 2):
            result = None
            for slot in range(slots):
                field = None
                first = 0
                for (members, _), table_ref in zip(groups, table_refs):
                    last = first + len(members)
                    value = jnp.concatenate(
                        [columns(slot, start + inner, first, last) for inner in range(2)],
                        axis=0,
                    )
                    value = right_dot(value, table_ref[...])
                    field = value if field is None else field + value
                    first = last
                field = field.reshape(2, rows_two, length)
                term = field * factors_ref[slot, start : start + 2]
                result = term if result is None else result + term
            if total is not None:
                result = result + refs[-2][start : start + 2]
            out_ref[start : start + 2] = result

    space = pl.BlockSpec((block, rows_two, length), lambda i: (i, 0, 0))
    operands = [factors] + tables + parts
    in_specs = (
        [pl.BlockSpec((slots, block, rows_two, length), lambda i: (0, i, 0, 0))]
        + [pl.BlockSpec(table.shape, lambda i: (0, 0)) for table in tables]
        + [
            pl.BlockSpec(part.shape[:3] + (block, rows_two), lambda i: (0, 0, 0, i, 0))
            for part in parts
        ]
    )
    if total is not None:
        operands.append(total)
        in_specs.append(space)
    size = rows_one * rows_two
    planes_count = sum(part.shape[0] * part.shape[2] for part in parts)
    return pl.pallas_call(
        body,
        grid=(rows_one // block,),
        in_specs=in_specs,
        out_specs=space,
        out_shape=jax.ShapeDtypeStruct((rows_one, rows_two, length), jnp.float32),
        compiler_params=params(),
        cost_estimate=pl.CostEstimate(
            flops=6 * slots * size * planes_count * length,
            bytes_accessed=4 * size * (slots * planes_count + (2 + slots) * length),
            transcendentals=0,
        ),
        name="backward_last",
    )(*operands)


def cosine_turns():
    points = np.cos(np.pi * (np.arange(64) + 0.5) / 64) * 0.125 + 0.125
    fit = np.polynomial.Polynomial.fit(
        points, np.cos(2.0 * np.pi * np.sqrt(points)), 8, domain=[0.0, 0.25]
    )
    return [float(value) for value in fit.convert().coef]


def cosine_factors(saved, chosen, scale):
    rows_one, rows_two, length = saved.shape
    slots = chosen.shape[0]
    block = min(8, rows_one)
    coefficients = cosine_turns()

    def body(chosen_ref, saved_ref, out_ref):
        for slot in range(slots):
            feature = chosen_ref[slot]
            turns = saved_ref[...] * (feature * (1.0 / 16.0))
            turns = turns - jnp.round(turns)
            square = turns * turns
            result = jnp.full_like(square, coefficients[-1])
            for value in coefficients[-2::-1]:
                result = result * square + value
            out_ref[slot] = result * (feature * (math.pi / 8.0 * scale))

    size = rows_one * rows_two * length
    return pl.pallas_call(
        body,
        grid=(rows_one // block,),
        in_specs=[
            pl.BlockSpec(memory_space=pltpu.SMEM),
            pl.BlockSpec((block, rows_two, length), lambda i: (i, 0, 0)),
        ],
        out_specs=pl.BlockSpec((slots, block, rows_two, length), lambda i: (0, i, 0, 0)),
        out_shape=jax.ShapeDtypeStruct((slots, rows_one, rows_two, length), jnp.float32),
        compiler_params=params(),
        cost_estimate=pl.CostEstimate(
            flops=24 * slots * size, bytes_accessed=4 * size * (1 + slots), transcendentals=0
        ),
        name="cosine_factors",
    )(chosen, saved)


def swap_pairs(width_px, half_px, delta):
    return [(px, px // half_px * half_px + (px % half_px ^ delta)) for px in range(width_px)]


def send_messages(message, width_px):
    half_px = width_px // 2
    if half_px <= 8:
        return [message[0]] + [
            lax.ppermute(message[delta], "px", swap_pairs(width_px, half_px, delta))
            for delta in range(1, half_px)
        ]
    groups = [list(range(half_px)), list(range(half_px, width_px))]
    index = lax.axis_index("px") % half_px ^ jnp.arange(half_px)
    message = jnp.take(jnp.stack(message), index, axis=0)
    message = lax.all_to_all(message, "px", 0, 0, axis_index_groups=groups, tiled=True)
    message = jnp.take(message, index, axis=0)
    return [message[delta] for delta in range(half_px)]


def message_rows(spectra, edge, select, count):
    slots, length_one, local_two, length_three = spectra.shape
    half_one = length_one // 2
    half_px = half_one // local_two
    padded = select.shape[0] // half_px
    used = slots * (local_two + 3)
    extent = used + -used % 8
    group = 4
    lanes = 128

    def body(spectra_ref, edge_ref, select_ref, *refs):
        flats = [ref.reshape(count * extent, half_one) for ref in refs[:half_px]]
        scratch = refs[half_px:]

        def chosen(value):
            return lax.dot_general(
                select_ref[...],
                value.astype(jnp.bfloat16),
                (((1,), (1,)), ((), ())),
                preferred_element_type=jnp.float32,
            )

        def store(value, row):
            for delta in range(half_px):
                flats[delta][pl.ds(row, count, stride=extent), :] = value[
                    delta * padded : delta * padded + count
                ]

        for slot in range(slots):
            for part, ref in enumerate(scratch):
                ref[...] = (
                    spectra_ref[slot, :half_one, :, part * lanes : (part + 1) * lanes]
                    .astype(jnp.float32)
                    .reshape(half_one * local_two, lanes)
                )
            for start in range(0, local_two, group):
                value = jnp.concatenate(
                    [
                        jnp.concatenate(
                            [
                                ref[pl.ds(start + inner, half_one, stride=local_two), :]
                                for ref in scratch
                            ],
                            axis=1,
                        )
                        for inner in range(group)
                    ],
                    axis=0,
                )
                value = chosen(value)
                for inner in range(group):
                    store(
                        value[:, inner * half_one : (inner + 1) * half_one],
                        slot * local_two + start + inner,
                    )
            first = slots * local_two + 3 * slot
            store(chosen(edge_ref[slot, :half_one]), first)
            tiled = jnp.concatenate([spectra_ref[slot, half_one]] * half_px, axis=0)
            value = chosen(tiled)
            row = lax.broadcasted_iota(jnp.int32, value.shape, 0) // padded
            lane = lax.broadcasted_iota(jnp.int32, value.shape, 1) // local_two
            store(jnp.where(row == lane, value, 0.0), first + 1)
            corner = edge_ref[slot, half_one : half_one + 1]
            store(chosen(jnp.broadcast_to(corner, (half_one, length_three))), first + 2)
        for flat in flats:
            for row in range(used, extent):
                flat[pl.ds(row, count, stride=extent), :] = jnp.zeros(
                    (count, half_one), jnp.float32
                )

    part = (slots, half_one + 1, local_two, length_three)
    return pl.pallas_call(
        body,
        grid=(1,),
        in_specs=[
            pl.BlockSpec(part, lambda i: (0, 0, 0, 0)),
            pl.BlockSpec(edge.shape, lambda i: (0, 0, 0)),
            pl.BlockSpec(select.shape, lambda i: (0, 0)),
        ],
        out_specs=[pl.BlockSpec((count, extent, half_one), lambda i: (0, 0, 0))] * half_px,
        out_shape=[jax.ShapeDtypeStruct((count, extent, half_one), jnp.float32)] * half_px,
        scratch_shapes=[pltpu.VMEM((half_one * local_two, lanes), jnp.float32)]
        * (length_three // lanes),
        compiler_params=params(),
        cost_estimate=pl.CostEstimate(
            flops=2 * slots * select.shape[0] * half_one * local_two * length_three,
            bytes_accessed=2 * math.prod(part) + 4 * half_px * count * extent * half_one,
            transcendentals=0,
        ),
        name="message_rows",
    )(spectra, edge, select)


def kernel_messages(spectra, edge, wanted, width_px, width_py):
    slots, length_one, local_two, length_three = spectra.shape
    half_one = length_one // 2
    half_px = width_px // 2
    count = wanted.shape[1]
    px_index = lax.axis_index("px")
    py_index = lax.axis_index("py")
    wanted = wanted.reshape(width_px, width_py, count)
    sources = np.arange(width_px)
    targets = np.stack(
        [sources // half_px * half_px + (sources % half_px ^ d) for d in range(half_px)],
        axis=1,
    )
    rows = jnp.asarray(wanted[targets].transpose(0, 2, 1, 3).reshape(-1, half_px * count))
    rows = rows[px_index * width_py + py_index]
    sublanes = 16
    if local_two % sublanes == 0:
        padded = count + -count % sublanes
        rows = rows.reshape(half_px, count)
        rows = jnp.pad(rows, ((0, 0), (0, padded - count)), constant_values=-1)
        rows = rows.reshape(-1)
        select = (rows[:, None] == jnp.arange(length_three)[None, :]).astype(jnp.bfloat16)
        return message_rows(spectra, edge, select, count)
    select = (rows[:, None] == jnp.arange(length_three)[None, :]).astype(jnp.bfloat16)
    chosen = jnp.einsum(
        "rk,jabk->rjba",
        select,
        spectra[:, : half_one + 1],
        preferred_element_type=jnp.float32,
    )
    chosen_edge = jnp.einsum(
        "rk,jak->rja",
        select.astype(jnp.float32),
        edge,
        precision=lax.Precision.HIGHEST,
        preferred_element_type=jnp.float32,
    )
    body = chosen[..., :half_one].reshape(half_px, count, slots * local_two, half_one)
    edge_two = chosen_edge[..., None, :half_one]
    corner = jnp.broadcast_to(chosen_edge[..., None, half_one:], edge_two.shape)
    last = chosen[..., half_one].reshape(half_px, count, slots, local_two)
    edge_one = jnp.stack(
        [
            jnp.pad(
                last[delta],
                (
                    (0, 0),
                    (0, 0),
                    (delta * local_two, (half_px - 1 - delta) * local_two),
                ),
            )
            for delta in range(half_px)
        ]
    )
    edge_one = edge_one.reshape(half_px * count, slots, 1, half_px * local_two)
    edges = jnp.concatenate([edge_two, edge_one, corner], axis=2)
    edges = edges.reshape(half_px, count, 3 * slots, half_one)
    spare = -(slots * (local_two + 3)) % 8
    message = jnp.concatenate([body, edges], axis=2)
    message = jnp.pad(message, ((0, 0), (0, 0), (0, spare), (0, 0)))
    return [message[delta] for delta in range(half_px)]


def on_device(adjoint, saved, spectra, freq_index, picked):
    width_px = lax.axis_size("px")
    width_py = lax.axis_size("py")
    px_index = lax.axis_index("px")
    py_index = lax.axis_index("py")
    devices = width_px * width_py
    half_px = width_px // 2
    half_devices = devices // 2
    half_index = px_index // half_px
    px_low = px_index % half_px
    rows_one, rows_two, length_three = adjoint.shape
    length_one = rows_one * width_px
    length_two = rows_two * width_py
    slots = picked.shape[0]

    order = paired_order(length_three)
    shared_depth = 8
    shared_chunks = SHARED if length_three % (8 * devices * SHARED) == 0 else 0
    shared_count = half_devices * shared_depth
    shared = [
        order[chunk * shared_count : (chunk + 1) * shared_count].reshape(half_devices, -1)
        for chunk in range(shared_chunks)
    ]
    single = order[shared_chunks * shared_count :].reshape(devices, -1)
    depth = single.shape[1]
    owned = [np.concatenate([chunk, chunk]) for chunk in shared] + [single]

    def folded_rows(members):
        folded = np.concatenate(members, axis=1)
        folded = np.minimum(folded, length_three - folded)
        distinct = [list(dict.fromkeys(row.tolist())) for row in folded]
        count = max(len(row) for row in distinct)
        wanted = np.array([row + [row[-1]] * (count - len(row)) for row in distinct])
        places = [[row.index(k) for k in ks] for row, ks in zip(distinct, folded)]
        return wanted, np.array(places)

    half_one = length_one // 2
    edge = lax.ppermute(
        spectra[:, : half_one + 1, 0].astype(jnp.float32),
        "px",
        [(0, half_px), (half_px, 0)],
    )
    last = hartley(length_three)

    def send(value, runs):
        depth = sum(run.shape[1] for run in runs)
        table = left_table(last[np.concatenate([run.reshape(-1) for run in runs])])
        copies = []
        row = 0
        place = 0
        for run in runs:
            for owner in range(run.shape[0]):
                owners = range(owner, devices, run.shape[0])
                planes = [target * depth + place for target in owners]
                copies.append((row, run.shape[1], planes))
                row += run.shape[1]
            place += run.shape[1]
        return forward_last(value, table, devices * depth, copies).reshape(
            devices, depth, rows_one, rows_two
        )

    sent = send(adjoint, shared[:1] + [single])

    def exchange(value):
        return lax.all_to_all(value, ("px", "py"), 0, 0, tiled=True)

    def arranged(value):
        return value.reshape(width_px, width_py, -1, rows_one, rows_two)

    barrier = lax.optimization_barrier
    device = px_index * width_py + py_index
    sent, spectra, edge, adjoint = barrier((sent, spectra, edge, adjoint))
    wanted, places = folded_rows(owned)
    messages = kernel_messages(spectra, edge, wanted, width_px, width_py)
    messages = send_messages(messages, width_px)
    places = jnp.asarray(places, dtype=jnp.int32)[device]
    local_two = length_two // width_px
    special = (px_low * local_two).astype(jnp.int32).reshape(1)

    order_one = np.arange(length_one // 2)
    order_one = np.concatenate([order_one, (length_one - order_one) % length_one])
    order_one[length_one // 2] = length_one // 2
    slabs = half_index * half_px + (px_low ^ jnp.arange(half_px))
    order_two = (slabs[:, None] * local_two + jnp.arange(local_two)[None, :]).reshape(-1)
    order_two = jnp.concatenate([order_two, partners(order_two, length_two)])
    one = hartley(length_one)[order_one]
    one_f = left_table(one)
    one_b = left_table(one.T)
    sites_two = jnp.arange(length_two)
    two_f = traced_table(sites_two, order_two, length_two, 0)
    two_b = traced_table(order_two, sites_two, length_two, 0)
    sites_half = (slabs[:, None] * rows_one + jnp.arange(rows_one)[None, :]).reshape(-1)
    half_one_b = traced_table(sites_half, jnp.asarray(order_one), length_one, 1)
    near_two = (sites_two + py_index * rows_two) % length_two
    near_two_b = traced_table(order_two, near_two, length_two, 0)
    tables = (one_f, two_f, one_b, two_b)
    half_tables = (one_f, two_f, half_one_b, near_two_b)

    feature_ids = jnp.arange(freq_index.shape[0], dtype=jnp.int32)
    chosen = jnp.sum(
        jnp.where(feature_ids[None, :] == picked[:, None], freq_index[None, :], 0), axis=1
    ).astype(jnp.float32)

    shared_source = (
        (px_low ^ jnp.arange(half_px))[None, :] * width_py
        + ((py_index - jnp.arange(width_py)) % width_py)[:, None]
    ).reshape(-1)

    def shared_fields(index, value):
        first = index * shared_depth
        return filter_planes(
            arranged(value),
            0,
            messages,
            places[first : first + shared_depth],
            special,
            half_tables,
            slots,
            True,
        )

    def shared_rows(pieces):
        return [pieces[0]] + [
            lax.ppermute(pieces[delta], "px", swap_pairs(width_px, half_px, delta))
            for delta in range(1, half_px)
        ]

    def shared_group(index, pieces):
        parts = [jnp.stack([piece[0] for piece in pieces])]
        for shift in range(1, width_py):
            pairs = [(c, (c + shift) % width_py) for c in range(width_py)]
            far = jnp.stack([piece[shift] for piece in pieces])
            parts.append(lax.ppermute(far, "py", pairs))
        return parts, shared_tables[index]

    shared_tables = []
    for chunk in shared:
        ids = jnp.asarray(chunk)[shared_source].reshape(-1)
        shared_tables.append(
            traced_table(ids, jnp.arange(length_three), length_three, 0)
        )
    scale = 1.0 / (length_one * length_two * length_three)
    single_table = right_table(last[single.reshape(-1)])
    first = shared_chunks * shared_depth

    def single_fields(value):
        return filter_planes(
            arranged(value),
            min(first, shared_depth),
            messages,
            places[first:],
            special,
            tables,
            slots,
            False,
        ).reshape(devices, slots, depth, rows_one, rows_two)

    factors = cosine_factors(saved, chosen, scale)
    if shared_chunks == 0:
        returned = exchange(single_fields(exchange(sent)))
        return backward_last([([returned], single_table)], factors, None)

    arrived = exchange(sent)
    sent = send(adjoint, shared[1:])
    sent, messages, places, tables, half_tables, shared_tables, factors = barrier(
        (sent, messages, places, tables, half_tables, shared_tables, factors)
    )
    arrived_late = exchange(sent)
    near = shared_rows(shared_fields(0, arrived))
    fields_single = single_fields(arrived)
    fields_single, near = barrier((fields_single, near))
    returned = exchange(fields_single)
    pieces = shared_fields(1, arrived_late)
    pieces, near = barrier((pieces, near))
    group = shared_group(0, near)
    late = shared_rows(pieces)
    total = backward_last([group], factors, None)
    late, total = barrier((late, total))
    return backward_last(
        [shared_group(1, late), ([returned], single_table)], factors, total
    )


def solution(mesh):
    placed = (
        P(("chain", "px"), "py", None),
        P(("chain", "px"), "py", None),
        P(None, None, "px", None),
        P(),
        P(),
    )
    return jax.shard_map(
        on_device,
        mesh=mesh,
        in_specs=placed,
        out_specs=P(("chain", "px"), "py", None),
        check_vma=False,
    )
```

```python
import math

import jax
import jax.numpy as jnp
import numpy as np
from jax import lax
from jax.experimental import pallas as pl
from jax.experimental.pallas import tpu as pltpu
from jax.sharding import PartitionSpec as P

VMEM_BYTES = 56 * 1024 * 1024
LAST_BYTES = 48 * 1024 * 1024
SHARED = 2
GROUP = 4


def hartley(length):
    counter = np.arange(length)
    angle = 2.0 * np.pi * ((counter[:, None] * counter[None, :]) % length) / length
    return np.cos(angle) + np.sin(angle)


def split_table(table):
    high = table.astype(np.float32).astype(jnp.bfloat16)
    low = (table - high.astype(np.float64)).astype(np.float32).astype(jnp.bfloat16)
    return high, low


def left_table(table):
    high, low = split_table(table)
    return jnp.asarray(np.concatenate([high, high, low], axis=1))


def right_table(table):
    high, low = split_table(table)
    return jnp.asarray(np.concatenate([high, high, low], axis=0))


def traced_table(rows, columns, length, axis):
    product = rows[:, None] * columns[None, :] % length
    angle = product.astype(jnp.float32) * (2.0 * math.pi / length)
    value = jnp.cos(angle) + jnp.sin(angle)
    high = lax.reduce_precision(value, 8, 7)
    low = value - high
    return jnp.concatenate([high, high, low], axis=axis).astype(jnp.bfloat16)


def partners(first, length):
    base = first % (length // 2) == 0
    return jnp.where(base, (first + length // 2) % length, (length - first) % length)


def paired_order(length):
    half = length // 2
    order = [0, half]
    for index in range(1, half):
        order += [index, length - index]
    return np.array(order)


def split_value(value):
    high = value.astype(jnp.bfloat16)
    low = (value - high.astype(jnp.float32)).astype(jnp.bfloat16)
    return high, low


def left_dot(table, value):
    high, low = split_value(value)
    stacked = jnp.concatenate([high, low, high], axis=0)
    return jnp.dot(table, stacked, preferred_element_type=jnp.float32)


def right_dot(value, table):
    high, low = split_value(value)
    stacked = jnp.concatenate([high, low, high], axis=1)
    return jnp.dot(stacked, table, preferred_element_type=jnp.float32)


def params(limit=VMEM_BYTES):
    return pltpu.CompilerParams(vmem_limit_bytes=limit)


def forward_last(adjoint, table, depth, copies):
    rows_one, rows_two, length = adjoint.shape
    count = table.shape[0]
    block = min(8, rows_one)

    def body(adjoint_ref, table_ref, out_ref):
        flat = out_ref.reshape(depth * block, rows_two)
        for start in range(0, block, 2):
            value = adjoint_ref[start : start + 2].reshape(2 * rows_two, length)
            high, low = split_value(value)
            stacked = jnp.concatenate([high, low, high], axis=1)
            result = lax.dot_general(
                table_ref[...],
                stacked,
                (((1,), (1,)), ((), ())),
                preferred_element_type=jnp.float32,
            )
            for inner in range(2):
                columns = slice(inner * rows_two, (inner + 1) * rows_two)
                for row, rows, planes in copies:
                    for plane in planes:
                        flat[
                            pl.ds(plane * block + start + inner, rows, stride=block), :
                        ] = result[row : row + rows, columns]

    return pl.pallas_call(
        body,
        grid=(rows_one // block,),
        in_specs=[
            pl.BlockSpec((block, rows_two, length), lambda i: (i, 0, 0)),
            pl.BlockSpec(table.shape, lambda i: (0, 0)),
        ],
        out_specs=pl.BlockSpec((depth, block, rows_two), lambda i: (0, i, 0)),
        out_shape=jax.ShapeDtypeStruct((depth, rows_one, rows_two), jnp.float32),
        compiler_params=params(),
        cost_estimate=pl.CostEstimate(
            flops=6 * count * rows_one * rows_two * length,
            bytes_accessed=4 * rows_one * rows_two * (length + depth),
            transcendentals=0,
        ),
        name="forward_last",
    )(adjoint, table)


def whole_plane(message_refs, slot, slots, special, local_two):
    blocks = [ref[0] for ref in message_refs]
    body = [block[slot * local_two : (slot + 1) * local_two] for block in blocks]
    folded = jnp.concatenate(body, axis=0)
    first = slots * local_two + 3 * slot
    edges = blocks[0][first : first + 3]
    for block in blocks[1:]:
        edges = edges + block[first : first + 3]
    edge_two, edge_one, corner = edges[0:1], edges[1:2], edges[2:3]
    extent = folded.shape
    row = lax.broadcasted_iota(jnp.int32, extent, 0)
    column = lax.broadcasted_iota(jnp.int32, extent, 1)
    right = jnp.where(row == special, edge_two, folded).T
    left = folded.T
    top = row == 0
    lower_left = jnp.where(top, edge_one, left)
    lower_right = jnp.where(top, jnp.where(column == special, corner, edge_one), right)
    return jnp.concatenate(
        [
            jnp.concatenate([left, right], axis=1),
            jnp.concatenate([lower_left, lower_right], axis=1),
        ],
        axis=0,
    )


def filter_planes(planes, first, messages, places, special, tables, slots, split):
    width_px, width_py, _, rows_one, rows_two = planes.shape
    planes_count = places.shape[0]
    length_one = width_px * rows_one
    length_two = width_py * rows_two
    out_px = tables[2].shape[0] // rows_one
    message_rows = messages[0].shape[1]
    local_two = length_two // 2 // len(messages)
    group = next(g for g in (GROUP, 2, 1) if planes_count % g == 0 and first % g == 0)

    def body(places_ref, special_ref, planes_ref, *refs):
        one_f, two_f, one_b, two_b = refs[group * len(messages) :][:4]
        out_refs = refs[group * len(messages) + 4 :]
        values = []
        for member in range(group):
            value = jnp.concatenate(
                [
                    planes_ref[:, part, member].reshape(length_one, rows_two)
                    for part in range(width_py)
                ],
                axis=1,
            )
            values.append(right_dot(value, two_f[...]))
        values = [left_dot(one_f[...], value) for value in values]
        for slot in range(slots):
            backs = []
            for member, value in enumerate(values):
                message_refs = refs[member * len(messages) : (member + 1) * len(messages)]
                plane = whole_plane(message_refs, slot, slots, special_ref[0], local_two)
                backs.append(left_dot(one_b[...], value * plane))
            for member, back in enumerate(backs):
                back = right_dot(back, two_b[...])
                for part in range(width_py):
                    piece = back[:, part * rows_two : (part + 1) * rows_two]
                    if split:
                        for index in range(out_px):
                            out_refs[index][part, slot, member] = piece[
                                index * rows_one : (index + 1) * rows_one
                            ]
                    else:
                        out_refs[0][:, part, slot, member] = piece.reshape(
                            out_px, rows_one, rows_two
                        )

    plane_size = length_one * length_two
    if split:
        extent = (width_py, slots, planes_count, rows_one, rows_two)
        out_shape = [jax.ShapeDtypeStruct(extent, jnp.float32)] * out_px
        out_specs = [
            pl.BlockSpec(
                (width_py, slots, group, rows_one, rows_two),
                lambda i, *_: (0, 0, i, 0, 0),
            )
        ] * out_px
    else:
        extent = (out_px, width_py, slots, planes_count, rows_one, rows_two)
        out_shape = [jax.ShapeDtypeStruct(extent, jnp.float32)]
        out_specs = [
            pl.BlockSpec(
                (out_px, width_py, slots, group, rows_one, rows_two),
                lambda i, *_: (0, 0, 0, i, 0, 0),
            )
        ]

    def message_spec(member):
        return pl.BlockSpec(
            (1, message_rows, length_one // 2),
            lambda i, places_ref, special_ref: (places_ref[group * i + member], 0, 0),
        )

    out_rows = out_px * rows_one
    outs = pl.pallas_call(
        body,
        grid_spec=pltpu.PrefetchScalarGridSpec(
            num_scalar_prefetch=2,
            grid=(planes_count // group,),
            in_specs=[
                pl.BlockSpec(
                    (width_px, width_py, group, rows_one, rows_two),
                    lambda i, *_: (0, 0, first // group + i, 0, 0),
                )
            ]
            + [message_spec(member) for member in range(group) for _ in messages]
            + [pl.BlockSpec(table.shape, lambda i, *_: (0, 0)) for table in tables],
            out_specs=out_specs,
        ),
        out_shape=out_shape,
        compiler_params=params(),
        cost_estimate=pl.CostEstimate(
            flops=6
            * planes_count
            * (
                plane_size * (length_one + length_two)
                + slots * out_rows * length_two * (length_one + length_two)
            ),
            bytes_accessed=4
            * planes_count
            * (plane_size + slots * (plane_size // 4 + out_rows * length_two)),
            transcendentals=0,
        ),
        name="filter_planes",
    )(places, special, planes, *(messages * group), *tables)
    return outs if split else outs[0]


def backward_last(groups, factors, total):
    parts = [part for members, _ in groups for part in members]
    tables = [table for _, table in groups]
    slots = factors.shape[0]
    rows_one, rows_two = parts[0].shape[3:]
    length = tables[0].shape[1]
    block = min(8, rows_one)

    def body(*refs):
        factors_ref = refs[0]
        table_refs = refs[1 : 1 + len(groups)]
        part_refs = refs[1 + len(groups) : 1 + len(groups) + len(parts)]
        out_ref = refs[-1]
        flats = [
            ref.reshape(math.prod(part.shape[:3]) * block, rows_two)
            for ref, part in zip(part_refs, parts)
        ]

        def columns(slot, site, first, last):
            found = []
            for index in range(first, last):
                sources, _, depth = parts[index].shape[:3]
                for source in range(sources):
                    row = (source * slots + slot) * depth * block + site
                    found.append(flats[index][pl.ds(row, depth, stride=block), :])
            return jnp.concatenate(found, axis=0).T

        for start in range(0, block, 2):
            result = None
            for slot in range(slots):
                field = None
                first = 0
                for (members, _), table_ref in zip(groups, table_refs):
                    last = first + len(members)
                    value = jnp.concatenate(
                        [columns(slot, start + inner, first, last) for inner in range(2)],
                        axis=0,
                    )
                    value = right_dot(value, table_ref[...])
                    field = value if field is None else field + value
                    first = last
                field = field.reshape(2, rows_two, length)
                term = field * factors_ref[slot, start : start + 2]
                result = term if result is None else result + term
            if total is not None:
                result = result + refs[-2][start : start + 2]
            out_ref[start : start + 2] = result

    space = pl.BlockSpec((block, rows_two, length), lambda i: (i, 0, 0))
    operands = [factors] + tables + parts
    in_specs = (
        [pl.BlockSpec((slots, block, rows_two, length), lambda i: (0, i, 0, 0))]
        + [pl.BlockSpec(table.shape, lambda i: (0, 0)) for table in tables]
        + [
            pl.BlockSpec(part.shape[:3] + (block, rows_two), lambda i: (0, 0, 0, i, 0))
            for part in parts
        ]
    )
    if total is not None:
        operands.append(total)
        in_specs.append(space)
    size = rows_one * rows_two
    planes_count = sum(part.shape[0] * part.shape[2] for part in parts)
    return pl.pallas_call(
        body,
        grid=(rows_one // block,),
        in_specs=in_specs,
        out_specs=space,
        out_shape=jax.ShapeDtypeStruct((rows_one, rows_two, length), jnp.float32),
        compiler_params=params(LAST_BYTES),
        cost_estimate=pl.CostEstimate(
            flops=6 * slots * size * planes_count * length,
            bytes_accessed=4 * size * (slots * planes_count + (2 + slots) * length),
            transcendentals=0,
        ),
        name="backward_last",
    )(*operands)


def cosine_turns():
    points = np.cos(np.pi * (np.arange(64) + 0.5) / 64) * 0.125 + 0.125
    fit = np.polynomial.Polynomial.fit(
        points, np.cos(2.0 * np.pi * np.sqrt(points)), 8, domain=[0.0, 0.25]
    )
    return [float(value) for value in fit.convert().coef]


def cosine_factors(saved, chosen, scale):
    rows_one, rows_two, length = saved.shape
    slots = chosen.shape[0]
    block = min(8, rows_one)
    coefficients = cosine_turns()

    def body(chosen_ref, saved_ref, out_ref):
        for slot in range(slots):
            feature = chosen_ref[slot]
            turns = saved_ref[...] * (feature * (1.0 / 16.0))
            turns = turns - jnp.round(turns)
            square = turns * turns
            result = jnp.full_like(square, coefficients[-1])
            for value in coefficients[-2::-1]:
                result = result * square + value
            out_ref[slot] = result * (feature * (math.pi / 8.0 * scale))

    size = rows_one * rows_two * length
    return pl.pallas_call(
        body,
        grid=(rows_one // block,),
        in_specs=[
            pl.BlockSpec(memory_space=pltpu.SMEM),
            pl.BlockSpec((block, rows_two, length), lambda i: (i, 0, 0)),
        ],
        out_specs=pl.BlockSpec((slots, block, rows_two, length), lambda i: (0, i, 0, 0)),
        out_shape=jax.ShapeDtypeStruct((slots, rows_one, rows_two, length), jnp.float32),
        compiler_params=params(),
        cost_estimate=pl.CostEstimate(
            flops=24 * slots * size, bytes_accessed=4 * size * (1 + slots), transcendentals=0
        ),
        name="cosine_factors",
    )(chosen, saved)


def swap_pairs(width_px, half_px, delta):
    return [(px, px // half_px * half_px + (px % half_px ^ delta)) for px in range(width_px)]


def send_messages(message, width_px):
    half_px = width_px // 2
    if half_px <= 8:
        return [message[0]] + [
            lax.ppermute(message[delta], "px", swap_pairs(width_px, half_px, delta))
            for delta in range(1, half_px)
        ]
    groups = [list(range(half_px)), list(range(half_px, width_px))]
    index = lax.axis_index("px") % half_px ^ jnp.arange(half_px)
    message = jnp.take(jnp.stack(message), index, axis=0)
    message = lax.all_to_all(message, "px", 0, 0, axis_index_groups=groups, tiled=True)
    message = jnp.take(message, index, axis=0)
    return [message[delta] for delta in range(half_px)]


def message_rows(spectra, edge, select, count):
    slots, length_one, local_two, length_three = spectra.shape
    half_one = length_one // 2
    half_px = half_one // local_two
    padded = select.shape[0] // half_px
    used = slots * (local_two + 3)
    extent = used + -used % 8
    group = 4
    lanes = 128

    def body(spectra_ref, edge_ref, select_ref, *refs):
        flats = [ref.reshape(count * extent, half_one) for ref in refs[:half_px]]
        scratch = refs[half_px:]

        def chosen(value):
            return lax.dot_general(
                select_ref[...],
                value.astype(jnp.bfloat16),
                (((1,), (1,)), ((), ())),
                preferred_element_type=jnp.float32,
            )

        def store(value, row):
            for delta in range(half_px):
                flats[delta][pl.ds(row, count, stride=extent), :] = value[
                    delta * padded : delta * padded + count
                ]

        for slot in range(slots):
            for part, ref in enumerate(scratch):
                ref[...] = (
                    spectra_ref[slot, :half_one, :, part * lanes : (part + 1) * lanes]
                    .astype(jnp.float32)
                    .reshape(half_one * local_two, lanes)
                )
            for start in range(0, local_two, group):
                value = jnp.concatenate(
                    [
                        jnp.concatenate(
                            [
                                ref[pl.ds(start + inner, half_one, stride=local_two), :]
                                for ref in scratch
                            ],
                            axis=1,
                        )
                        for inner in range(group)
                    ],
                    axis=0,
                )
                value = chosen(value)
                for inner in range(group):
                    store(
                        value[:, inner * half_one : (inner + 1) * half_one],
                        slot * local_two + start + inner,
                    )
            first = slots * local_two + 3 * slot
            store(chosen(edge_ref[slot, :half_one]), first)
            tiled = jnp.concatenate([spectra_ref[slot, half_one]] * half_px, axis=0)
            value = chosen(tiled)
            row = lax.broadcasted_iota(jnp.int32, value.shape, 0) // padded
            lane = lax.broadcasted_iota(jnp.int32, value.shape, 1) // local_two
            store(jnp.where(row == lane, value, 0.0), first + 1)
            corner = edge_ref[slot, half_one : half_one + 1]
            store(chosen(jnp.broadcast_to(corner, (half_one, length_three))), first + 2)
        for flat in flats:
            for row in range(used, extent):
                flat[pl.ds(row, count, stride=extent), :] = jnp.zeros(
                    (count, half_one), jnp.float32
                )

    part = (slots, half_one + 1, local_two, length_three)
    return pl.pallas_call(
        body,
        grid=(1,),
        in_specs=[
            pl.BlockSpec(part, lambda i: (0, 0, 0, 0)),
            pl.BlockSpec(edge.shape, lambda i: (0, 0, 0)),
            pl.BlockSpec(select.shape, lambda i: (0, 0)),
        ],
        out_specs=[pl.BlockSpec((count, extent, half_one), lambda i: (0, 0, 0))] * half_px,
        out_shape=[jax.ShapeDtypeStruct((count, extent, half_one), jnp.float32)] * half_px,
        scratch_shapes=[pltpu.VMEM((half_one * local_two, lanes), jnp.float32)]
        * (length_three // lanes),
        compiler_params=params(),
        cost_estimate=pl.CostEstimate(
            flops=2 * slots * select.shape[0] * half_one * local_two * length_three,
            bytes_accessed=2 * math.prod(part) + 4 * half_px * count * extent * half_one,
            transcendentals=0,
        ),
        name="message_rows",
    )(spectra, edge, select)


def kernel_messages(spectra, edge, wanted, width_px, width_py):
    slots, length_one, local_two, length_three = spectra.shape
    half_one = length_one // 2
    half_px = width_px // 2
    count = wanted.shape[1]
    px_index = lax.axis_index("px")
    py_index = lax.axis_index("py")
    wanted = wanted.reshape(width_px, width_py, count)
    sources = np.arange(width_px)
    targets = np.stack(
        [sources // half_px * half_px + (sources % half_px ^ d) for d in range(half_px)],
        axis=1,
    )
    rows = jnp.asarray(wanted[targets].transpose(0, 2, 1, 3).reshape(-1, half_px * count))
    rows = rows[px_index * width_py + py_index]
    sublanes = 16
    if local_two % sublanes == 0:
        padded = count + -count % sublanes
        rows = rows.reshape(half_px, count)
        rows = jnp.pad(rows, ((0, 0), (0, padded - count)), constant_values=-1)
        rows = rows.reshape(-1)
        select = (rows[:, None] == jnp.arange(length_three)[None, :]).astype(jnp.bfloat16)
        return message_rows(spectra, edge, select, count)
    select = (rows[:, None] == jnp.arange(length_three)[None, :]).astype(jnp.bfloat16)
    chosen = jnp.einsum(
        "rk,jabk->rjba",
        select,
        spectra[:, : half_one + 1],
        preferred_element_type=jnp.float32,
    )
    chosen_edge = jnp.einsum(
        "rk,jak->rja",
        select.astype(jnp.float32),
        edge,
        precision=lax.Precision.HIGHEST,
        preferred_element_type=jnp.float32,
    )
    body = chosen[..., :half_one].reshape(half_px, count, slots * local_two, half_one)
    edge_two = chosen_edge[..., None, :half_one]
    corner = jnp.broadcast_to(chosen_edge[..., None, half_one:], edge_two.shape)
    last = chosen[..., half_one].reshape(half_px, count, slots, local_two)
    edge_one = jnp.stack(
        [
            jnp.pad(
                last[delta],
                (
                    (0, 0),
                    (0, 0),
                    (delta * local_two, (half_px - 1 - delta) * local_two),
                ),
            )
            for delta in range(half_px)
        ]
    )
    edge_one = edge_one.reshape(half_px * count, slots, 1, half_px * local_two)
    edges = jnp.concatenate([edge_two, edge_one, corner], axis=2)
    edges = edges.reshape(half_px, count, 3 * slots, half_one)
    spare = -(slots * (local_two + 3)) % 8
    message = jnp.concatenate([body, edges], axis=2)
    message = jnp.pad(message, ((0, 0), (0, 0), (0, spare), (0, 0)))
    return [message[delta] for delta in range(half_px)]


def on_device(adjoint, saved, spectra, freq_index, picked):
    width_px = lax.axis_size("px")
    width_py = lax.axis_size("py")
    px_index = lax.axis_index("px")
    py_index = lax.axis_index("py")
    devices = width_px * width_py
    half_px = width_px // 2
    half_devices = devices // 2
    half_index = px_index // half_px
    px_low = px_index % half_px
    rows_one, rows_two, length_three = adjoint.shape
    length_one = rows_one * width_px
    length_two = rows_two * width_py
    slots = picked.shape[0]

    order = paired_order(length_three)
    shared_depth = 8
    shared_chunks = SHARED if length_three % (8 * devices * SHARED) == 0 else 0
    shared_count = half_devices * shared_depth
    shared = [
        order[chunk * shared_count : (chunk + 1) * shared_count].reshape(half_devices, -1)
        for chunk in range(shared_chunks)
    ]
    single = order[shared_chunks * shared_count :].reshape(devices, -1)
    depth = single.shape[1]
    owned = [np.concatenate([chunk, chunk]) for chunk in shared] + [single]

    def folded_rows(members):
        folded = np.concatenate(members, axis=1)
        folded = np.minimum(folded, length_three - folded)
        distinct = [list(dict.fromkeys(row.tolist())) for row in folded]
        count = max(len(row) for row in distinct)
        wanted = np.array([row + [row[-1]] * (count - len(row)) for row in distinct])
        places = [[row.index(k) for k in ks] for row, ks in zip(distinct, folded)]
        return wanted, np.array(places)

    half_one = length_one // 2
    edge = lax.ppermute(
        spectra[:, : half_one + 1, 0].astype(jnp.float32),
        "px",
        [(0, half_px), (half_px, 0)],
    )
    last = hartley(length_three)

    def send(value, runs):
        depth = sum(run.shape[1] for run in runs)
        table = left_table(last[np.concatenate([run.reshape(-1) for run in runs])])
        copies = []
        row = 0
        place = 0
        for run in runs:
            for owner in range(run.shape[0]):
                owners = range(owner, devices, run.shape[0])
                planes = [target * depth + place for target in owners]
                copies.append((row, run.shape[1], planes))
                row += run.shape[1]
            place += run.shape[1]
        return forward_last(value, table, devices * depth, copies).reshape(
            devices, depth, rows_one, rows_two
        )

    sent = send(adjoint, shared[:1] + [single])

    def exchange(value):
        return lax.all_to_all(value, ("px", "py"), 0, 0, tiled=True)

    def arranged(value):
        return value.reshape(width_px, width_py, -1, rows_one, rows_two)

    barrier = lax.optimization_barrier
    device = px_index * width_py + py_index
    sent, spectra, edge, adjoint = barrier((sent, spectra, edge, adjoint))
    wanted, places = folded_rows(owned)
    messages = kernel_messages(spectra, edge, wanted, width_px, width_py)
    messages, saved, adjoint, px_index, py_index = barrier(
        (messages, saved, adjoint, px_index, py_index)
    )
    half_index = px_index // half_px
    px_low = px_index % half_px
    messages = send_messages(messages, width_px)
    places = jnp.asarray(places, dtype=jnp.int32)[device]
    local_two = length_two // width_px
    special = (px_low * local_two).astype(jnp.int32).reshape(1)

    order_one = np.arange(length_one // 2)
    order_one = np.concatenate([order_one, (length_one - order_one) % length_one])
    order_one[length_one // 2] = length_one // 2
    slabs = half_index * half_px + (px_low ^ jnp.arange(half_px))
    order_two = (slabs[:, None] * local_two + jnp.arange(local_two)[None, :]).reshape(-1)
    order_two = jnp.concatenate([order_two, partners(order_two, length_two)])
    one = hartley(length_one)[order_one]
    one_f = left_table(one)
    one_b = left_table(one.T)
    sites_two = jnp.arange(length_two)
    two_f = traced_table(sites_two, order_two, length_two, 0)
    two_b = traced_table(order_two, sites_two, length_two, 0)
    sites_half = (slabs[:, None] * rows_one + jnp.arange(rows_one)[None, :]).reshape(-1)
    half_one_b = traced_table(sites_half, jnp.asarray(order_one), length_one, 1)
    near_two = (sites_two + py_index * rows_two) % length_two
    near_two_b = traced_table(order_two, near_two, length_two, 0)
    tables = (one_f, two_f, one_b, two_b)
    half_tables = (one_f, two_f, half_one_b, near_two_b)

    feature_ids = jnp.arange(freq_index.shape[0], dtype=jnp.int32)
    chosen = jnp.sum(
        jnp.where(feature_ids[None, :] == picked[:, None], freq_index[None, :], 0), axis=1
    ).astype(jnp.float32)

    shared_source = (
        (px_low ^ jnp.arange(half_px))[None, :] * width_py
        + ((py_index - jnp.arange(width_py)) % width_py)[:, None]
    ).reshape(-1)

    def shared_fields(index, value):
        first = index * shared_depth
        return filter_planes(
            arranged(value),
            0,
            messages,
            places[first : first + shared_depth],
            special,
            half_tables,
            slots,
            True,
        )

    def shared_rows(pieces):
        return [pieces[0]] + [
            lax.ppermute(pieces[delta], "px", swap_pairs(width_px, half_px, delta))
            for delta in range(1, half_px)
        ]

    def shared_group(index, pieces):
        parts = [jnp.stack([piece[0] for piece in pieces])]
        for shift in range(1, width_py):
            pairs = [(c, (c + shift) % width_py) for c in range(width_py)]
            far = jnp.stack([piece[shift] for piece in pieces])
            parts.append(lax.ppermute(far, "py", pairs))
        return parts, shared_tables[index]

    shared_tables = []
    for chunk in shared:
        ids = jnp.asarray(chunk)[shared_source].reshape(-1)
        shared_tables.append(
            traced_table(ids, jnp.arange(length_three), length_three, 0)
        )
    scale = 1.0 / (length_one * length_two * length_three)
    single_table = right_table(last[single.reshape(-1)])
    first = shared_chunks * shared_depth

    def single_fields(value):
        return filter_planes(
            arranged(value),
            min(first, shared_depth),
            messages,
            places[first:],
            special,
            tables,
            slots,
            False,
        ).reshape(devices, slots, depth, rows_one, rows_two)

    factors = cosine_factors(saved, chosen, scale)
    if shared_chunks == 0:
        returned = exchange(single_fields(exchange(sent)))
        return backward_last([([returned], single_table)], factors, None)

    arrived = exchange(sent)
    sent = send(adjoint, shared[1:])
    sent, messages, places, tables, half_tables, shared_tables, factors = barrier(
        (sent, messages, places, tables, half_tables, shared_tables, factors)
    )
    arrived_late = exchange(sent)
    near = shared_rows(shared_fields(0, arrived))
    fields_single = single_fields(arrived)
    fields_single, near = barrier((fields_single, near))
    returned = exchange(fields_single)
    pieces = shared_fields(1, arrived_late)
    pieces, near = barrier((pieces, near))
    group = shared_group(0, near)
    late = shared_rows(pieces)
    total = backward_last([group], factors, None)
    late, total = barrier((late, total))
    return backward_last(
        [shared_group(1, late), ([returned], single_table)], factors, total
    )


def solution(mesh):
    placed = (
        P(("chain", "px"), "py", None),
        P(("chain", "px"), "py", None),
        P(None, None, "px", None),
        P(),
        P(),
    )
    return jax.shard_map(
        on_device,
        mesh=mesh,
        in_specs=placed,
        out_specs=P(("chain", "px"), "py", None),
        check_vma=False,
    )
```

```python
import math

import jax
import jax.numpy as jnp
import numpy as np
from jax import lax
from jax.experimental import pallas as pl
from jax.experimental.pallas import tpu as pltpu
from jax.sharding import PartitionSpec as P

VMEM_BYTES = 56 * 1024 * 1024
LAST_BYTES = 48 * 1024 * 1024
SHARED = 2
GROUP = 4


def hartley(length):
    counter = np.arange(length)
    angle = 2.0 * np.pi * ((counter[:, None] * counter[None, :]) % length) / length
    return np.cos(angle) + np.sin(angle)


def split_table(table):
    high = table.astype(np.float32).astype(jnp.bfloat16)
    low = (table - high.astype(np.float64)).astype(np.float32).astype(jnp.bfloat16)
    return high, low


def left_table(table):
    high, low = split_table(table)
    return jnp.asarray(np.concatenate([high, high, low], axis=1))


def right_table(table):
    high, low = split_table(table)
    return jnp.asarray(np.concatenate([high, high, low], axis=0))


def traced_table(rows, columns, length, axis):
    product = rows[:, None] * columns[None, :] % length
    angle = product.astype(jnp.float32) * (2.0 * math.pi / length)
    value = jnp.cos(angle) + jnp.sin(angle)
    high = lax.reduce_precision(value, 8, 7)
    low = value - high
    return jnp.concatenate([high, high, low], axis=axis).astype(jnp.bfloat16)


def partners(first, length):
    base = first % (length // 2) == 0
    return jnp.where(base, (first + length // 2) % length, (length - first) % length)


def paired_order(length):
    half = length // 2
    order = [0, half]
    for index in range(1, half):
        order += [index, length - index]
    return np.array(order)


def split_value(value):
    high = value.astype(jnp.bfloat16)
    low = (value - high.astype(jnp.float32)).astype(jnp.bfloat16)
    return high, low


def left_dot(table, value):
    high, low = split_value(value)
    stacked = jnp.concatenate([high, low, high], axis=0)
    return jnp.dot(table, stacked, preferred_element_type=jnp.float32)


def right_dot(value, table):
    high, low = split_value(value)
    stacked = jnp.concatenate([high, low, high], axis=1)
    return jnp.dot(stacked, table, preferred_element_type=jnp.float32)


def params(limit=VMEM_BYTES):
    return pltpu.CompilerParams(vmem_limit_bytes=limit)


def forward_last(adjoint, table, depth, copies):
    rows_one, rows_two, length = adjoint.shape
    count = table.shape[0]
    block = min(8, rows_one)

    def body(adjoint_ref, table_ref, out_ref):
        flat = out_ref.reshape(depth * block, rows_two)
        for start in range(0, block, 2):
            value = adjoint_ref[start : start + 2].reshape(2 * rows_two, length)
            high, low = split_value(value)
            stacked = jnp.concatenate([high, low, high], axis=1)
            result = lax.dot_general(
                table_ref[...],
                stacked,
                (((1,), (1,)), ((), ())),
                preferred_element_type=jnp.float32,
            )
            for inner in range(2):
                columns = slice(inner * rows_two, (inner + 1) * rows_two)
                for row, rows, planes in copies:
                    for plane in planes:
                        flat[
                            pl.ds(plane * block + start + inner, rows, stride=block), :
                        ] = result[row : row + rows, columns]

    return pl.pallas_call(
        body,
        grid=(rows_one // block,),
        in_specs=[
            pl.BlockSpec((block, rows_two, length), lambda i: (i, 0, 0)),
            pl.BlockSpec(table.shape, lambda i: (0, 0)),
        ],
        out_specs=pl.BlockSpec((depth, block, rows_two), lambda i: (0, i, 0)),
        out_shape=jax.ShapeDtypeStruct((depth, rows_one, rows_two), jnp.float32),
        compiler_params=params(),
        cost_estimate=pl.CostEstimate(
            flops=6 * count * rows_one * rows_two * length,
            bytes_accessed=4 * rows_one * rows_two * (length + depth),
            transcendentals=0,
        ),
        name="forward_last",
    )(adjoint, table)


def whole_plane(message_refs, slot, slots, special, local_two):
    blocks = [ref[0] for ref in message_refs]
    body = [block[slot * local_two : (slot + 1) * local_two] for block in blocks]
    folded = jnp.concatenate(body, axis=0)
    first = slots * local_two + 3 * slot
    edges = blocks[0][first : first + 3]
    for block in blocks[1:]:
        edges = edges + block[first : first + 3]
    edge_two, edge_one, corner = edges[0:1], edges[1:2], edges[2:3]
    extent = folded.shape
    row = lax.broadcasted_iota(jnp.int32, extent, 0)
    column = lax.broadcasted_iota(jnp.int32, extent, 1)
    right = jnp.where(row == special, edge_two, folded).T
    left = folded.T
    top = row == 0
    lower_left = jnp.where(top, edge_one, left)
    lower_right = jnp.where(top, jnp.where(column == special, corner, edge_one), right)
    return jnp.concatenate(
        [
            jnp.concatenate([left, right], axis=1),
            jnp.concatenate([lower_left, lower_right], axis=1),
        ],
        axis=0,
    )


def filter_planes(planes, first, messages, places, special, tables, slots, split):
    width_px, width_py, _, rows_one, rows_two = planes.shape
    planes_count = places.shape[0]
    length_one = width_px * rows_one
    length_two = width_py * rows_two
    out_px = tables[2].shape[0] // rows_one
    message_rows = messages[0].shape[1]
    local_two = length_two // 2 // len(messages)
    group = next(g for g in (GROUP, 2, 1) if planes_count % g == 0 and first % g == 0)

    def body(places_ref, special_ref, planes_ref, *refs):
        one_f, two_f, one_b, two_b = refs[group * len(messages) :][:4]
        out_refs = refs[group * len(messages) + 4 :]
        values = []
        for member in range(group):
            value = jnp.concatenate(
                [
                    planes_ref[:, part, member].reshape(length_one, rows_two)
                    for part in range(width_py)
                ],
                axis=1,
            )
            values.append(right_dot(value, two_f[...]))
        values = [left_dot(one_f[...], value) for value in values]
        for slot in range(slots):
            backs = []
            for member, value in enumerate(values):
                message_refs = refs[member * len(messages) : (member + 1) * len(messages)]
                plane = whole_plane(message_refs, slot, slots, special_ref[0], local_two)
                backs.append(left_dot(one_b[...], value * plane))
            for member, back in enumerate(backs):
                back = right_dot(back, two_b[...])
                for part in range(width_py):
                    piece = back[:, part * rows_two : (part + 1) * rows_two]
                    if split:
                        for index in range(out_px):
                            out_refs[index][part, slot, member] = piece[
                                index * rows_one : (index + 1) * rows_one
                            ]
                    else:
                        out_refs[0][:, part, slot, member] = piece.reshape(
                            out_px, rows_one, rows_two
                        )

    plane_size = length_one * length_two
    if split:
        extent = (width_py, slots, planes_count, rows_one, rows_two)
        out_shape = [jax.ShapeDtypeStruct(extent, jnp.float32)] * out_px
        out_specs = [
            pl.BlockSpec(
                (width_py, slots, group, rows_one, rows_two),
                lambda i, *_: (0, 0, i, 0, 0),
            )
        ] * out_px
    else:
        extent = (out_px, width_py, slots, planes_count, rows_one, rows_two)
        out_shape = [jax.ShapeDtypeStruct(extent, jnp.float32)]
        out_specs = [
            pl.BlockSpec(
                (out_px, width_py, slots, group, rows_one, rows_two),
                lambda i, *_: (0, 0, 0, i, 0, 0),
            )
        ]

    def message_spec(member):
        return pl.BlockSpec(
            (1, message_rows, length_one // 2),
            lambda i, places_ref, special_ref: (places_ref[group * i + member], 0, 0),
        )

    out_rows = out_px * rows_one
    outs = pl.pallas_call(
        body,
        grid_spec=pltpu.PrefetchScalarGridSpec(
            num_scalar_prefetch=2,
            grid=(planes_count // group,),
            in_specs=[
                pl.BlockSpec(
                    (width_px, width_py, group, rows_one, rows_two),
                    lambda i, *_: (0, 0, first // group + i, 0, 0),
                )
            ]
            + [message_spec(member) for member in range(group) for _ in messages]
            + [pl.BlockSpec(table.shape, lambda i, *_: (0, 0)) for table in tables],
            out_specs=out_specs,
        ),
        out_shape=out_shape,
        compiler_params=params(),
        cost_estimate=pl.CostEstimate(
            flops=6
            * planes_count
            * (
                plane_size * (length_one + length_two)
                + slots * out_rows * length_two * (length_one + length_two)
            ),
            bytes_accessed=4
            * planes_count
            * (plane_size + slots * (plane_size // 4 + out_rows * length_two)),
            transcendentals=0,
        ),
        name="filter_planes",
    )(places, special, planes, *(messages * group), *tables)
    return outs if split else outs[0]


def backward_last(groups, factors, total):
    parts = [part for members, _ in groups for part in members]
    tables = [table for _, table in groups]
    slots = factors.shape[0]
    rows_one, rows_two = parts[0].shape[3:]
    length = tables[0].shape[1]
    block = min(8, rows_one)

    def body(*refs):
        factors_ref = refs[0]
        table_refs = refs[1 : 1 + len(groups)]
        part_refs = refs[1 + len(groups) : 1 + len(groups) + len(parts)]
        out_ref = refs[-1]
        flats = [
            ref.reshape(math.prod(part.shape[:3]) * block, rows_two)
            for ref, part in zip(part_refs, parts)
        ]

        def columns(slot, site, first, last):
            found = []
            for index in range(first, last):
                sources, _, depth = parts[index].shape[:3]
                for source in range(sources):
                    row = (source * slots + slot) * depth * block + site
                    found.append(flats[index][pl.ds(row, depth, stride=block), :])
            value = jnp.concatenate(found, axis=0)
            if value.shape[0] * 2 != rows_two:
                return value.T
            high = value.astype(jnp.bfloat16).astype(jnp.float32)
            return jnp.concatenate([high, value - high], axis=0).T

        for start in range(0, block, 2):
            result = None
            for slot in range(slots):
                field = None
                first = 0
                for (members, _), table_ref in zip(groups, table_refs):
                    last = first + len(members)
                    value = jnp.concatenate(
                        [columns(slot, start + inner, first, last) for inner in range(2)],
                        axis=0,
                    )
                    if value.shape[1] * 3 == table_ref.shape[0]:
                        value = right_dot(value, table_ref[...])
                    else:
                        value = value.astype(jnp.bfloat16)
                        value = jnp.dot(
                            jnp.concatenate([value, value], axis=1),
                            jnp.concatenate(
                                [table_ref[...], jnp.zeros_like(table_ref[: value.shape[1] // 2])],
                                axis=0,
                            ),
                            preferred_element_type=jnp.float32,
                        )
                    field = value if field is None else field + value
                    first = last
                field = field.reshape(2, rows_two, length)
                term = field * factors_ref[slot, start : start + 2]
                result = term if result is None else result + term
            if total is not None:
                result = result + refs[-2][start : start + 2]
            out_ref[start : start + 2] = result

    space = pl.BlockSpec((block, rows_two, length), lambda i: (i, 0, 0))
    operands = [factors] + tables + parts
    in_specs = (
        [pl.BlockSpec((slots, block, rows_two, length), lambda i: (0, i, 0, 0))]
        + [pl.BlockSpec(table.shape, lambda i: (0, 0)) for table in tables]
        + [
            pl.BlockSpec(part.shape[:3] + (block, rows_two), lambda i: (0, 0, 0, i, 0))
            for part in parts
        ]
    )
    if total is not None:
        operands.append(total)
        in_specs.append(space)
    size = rows_one * rows_two
    planes_count = sum(part.shape[0] * part.shape[2] for part in parts)
    return pl.pallas_call(
        body,
        grid=(rows_one // block,),
        in_specs=in_specs,
        out_specs=space,
        out_shape=jax.ShapeDtypeStruct((rows_one, rows_two, length), jnp.float32),
        compiler_params=params(LAST_BYTES),
        cost_estimate=pl.CostEstimate(
            flops=6 * slots * size * planes_count * length,
            bytes_accessed=4 * size * (slots * planes_count + (2 + slots) * length),
            transcendentals=0,
        ),
        name="backward_last",
    )(*operands)


def cosine_turns():
    points = np.cos(np.pi * (np.arange(64) + 0.5) / 64) * 0.125 + 0.125
    fit = np.polynomial.Polynomial.fit(
        points, np.cos(2.0 * np.pi * np.sqrt(points)), 8, domain=[0.0, 0.25]
    )
    return [float(value) for value in fit.convert().coef]


def cosine_factors(saved, chosen, scale):
    rows_one, rows_two, length = saved.shape
    slots = chosen.shape[0]
    block = min(8, rows_one)
    coefficients = cosine_turns()

    def body(chosen_ref, saved_ref, out_ref):
        for slot in range(slots):
            feature = chosen_ref[slot]
            turns = saved_ref[...] * (feature * (1.0 / 16.0))
            turns = turns - jnp.round(turns)
            square = turns * turns
            result = jnp.full_like(square, coefficients[-1])
            for value in coefficients[-2::-1]:
                result = result * square + value
            out_ref[slot] = result * (feature * (math.pi / 8.0 * scale))

    size = rows_one * rows_two * length
    return pl.pallas_call(
        body,
        grid=(rows_one // block,),
        in_specs=[
            pl.BlockSpec(memory_space=pltpu.SMEM),
            pl.BlockSpec((block, rows_two, length), lambda i: (i, 0, 0)),
        ],
        out_specs=pl.BlockSpec((slots, block, rows_two, length), lambda i: (0, i, 0, 0)),
        out_shape=jax.ShapeDtypeStruct((slots, rows_one, rows_two, length), jnp.float32),
        compiler_params=params(),
        cost_estimate=pl.CostEstimate(
            flops=24 * slots * size, bytes_accessed=4 * size * (1 + slots), transcendentals=0
        ),
        name="cosine_factors",
    )(chosen, saved)


def swap_pairs(width_px, half_px, delta):
    return [(px, px // half_px * half_px + (px % half_px ^ delta)) for px in range(width_px)]


def send_messages(message, width_px):
    half_px = width_px // 2
    if half_px <= 8:
        return [message[0]] + [
            lax.ppermute(message[delta], "px", swap_pairs(width_px, half_px, delta))
            for delta in range(1, half_px)
        ]
    groups = [list(range(half_px)), list(range(half_px, width_px))]
    index = lax.axis_index("px") % half_px ^ jnp.arange(half_px)
    message = jnp.take(jnp.stack(message), index, axis=0)
    message = lax.all_to_all(message, "px", 0, 0, axis_index_groups=groups, tiled=True)
    message = jnp.take(message, index, axis=0)
    return [message[delta] for delta in range(half_px)]


def message_rows(spectra, edge, select, count):
    slots, length_one, local_two, length_three = spectra.shape
    half_one = length_one // 2
    half_px = half_one // local_two
    padded = select.shape[0] // half_px
    used = slots * (local_two + 3)
    extent = used + -used % 8
    group = 4
    lanes = 128

    def body(spectra_ref, edge_ref, select_ref, *refs):
        flats = [ref.reshape(count * extent, half_one) for ref in refs[:half_px]]
        scratch = refs[half_px:]

        def chosen(value):
            return lax.dot_general(
                select_ref[...],
                value.astype(jnp.bfloat16),
                (((1,), (1,)), ((), ())),
                preferred_element_type=jnp.float32,
            )

        def store(value, row):
            for delta in range(half_px):
                flats[delta][pl.ds(row, count, stride=extent), :] = value[
                    delta * padded : delta * padded + count
                ]

        for slot in range(slots):
            for part, ref in enumerate(scratch):
                ref[...] = (
                    spectra_ref[slot, :half_one, :, part * lanes : (part + 1) * lanes]
                    .astype(jnp.float32)
                    .reshape(half_one * local_two, lanes)
                )
            for start in range(0, local_two, group):
                value = jnp.concatenate(
                    [
                        jnp.concatenate(
                            [
                                ref[pl.ds(start + inner, half_one, stride=local_two), :]
                                for ref in scratch
                            ],
                            axis=1,
                        )
                        for inner in range(group)
                    ],
                    axis=0,
                )
                value = chosen(value)
                for inner in range(group):
                    store(
                        value[:, inner * half_one : (inner + 1) * half_one],
                        slot * local_two + start + inner,
                    )
            first = slots * local_two + 3 * slot
            store(chosen(edge_ref[slot, :half_one]), first)
            tiled = jnp.concatenate([spectra_ref[slot, half_one]] * half_px, axis=0)
            value = chosen(tiled)
            row = lax.broadcasted_iota(jnp.int32, value.shape, 0) // padded
            lane = lax.broadcasted_iota(jnp.int32, value.shape, 1) // local_two
            store(jnp.where(row == lane, value, 0.0), first + 1)
            corner = edge_ref[slot, half_one : half_one + 1]
            store(chosen(jnp.broadcast_to(corner, (half_one, length_three))), first + 2)
        for flat in flats:
            for row in range(used, extent):
                flat[pl.ds(row, count, stride=extent), :] = jnp.zeros(
                    (count, half_one), jnp.float32
                )

    part = (slots, half_one + 1, local_two, length_three)
    return pl.pallas_call(
        body,
        grid=(1,),
        in_specs=[
            pl.BlockSpec(part, lambda i: (0, 0, 0, 0)),
            pl.BlockSpec(edge.shape, lambda i: (0, 0, 0)),
            pl.BlockSpec(select.shape, lambda i: (0, 0)),
        ],
        out_specs=[pl.BlockSpec((count, extent, half_one), lambda i: (0, 0, 0))] * half_px,
        out_shape=[jax.ShapeDtypeStruct((count, extent, half_one), jnp.float32)] * half_px,
        scratch_shapes=[pltpu.VMEM((half_one * local_two, lanes), jnp.float32)]
        * (length_three // lanes),
        compiler_params=params(),
        cost_estimate=pl.CostEstimate(
            flops=2 * slots * select.shape[0] * half_one * local_two * length_three,
            bytes_accessed=2 * math.prod(part) + 4 * half_px * count * extent * half_one,
            transcendentals=0,
        ),
        name="message_rows",
    )(spectra, edge, select)


def kernel_messages(spectra, edge, wanted, width_px, width_py):
    slots, length_one, local_two, length_three = spectra.shape
    half_one = length_one // 2
    half_px = width_px // 2
    count = wanted.shape[1]
    px_index = lax.axis_index("px")
    py_index = lax.axis_index("py")
    wanted = wanted.reshape(width_px, width_py, count)
    sources = np.arange(width_px)
    targets = np.stack(
        [sources // half_px * half_px + (sources % half_px ^ d) for d in range(half_px)],
        axis=1,
    )
    rows = jnp.asarray(wanted[targets].transpose(0, 2, 1, 3).reshape(-1, half_px * count))
    rows = rows[px_index * width_py + py_index]
    sublanes = 16
    if local_two % sublanes == 0:
        padded = count + -count % sublanes
        rows = rows.reshape(half_px, count)
        rows = jnp.pad(rows, ((0, 0), (0, padded - count)), constant_values=-1)
        rows = rows.reshape(-1)
        select = (rows[:, None] == jnp.arange(length_three)[None, :]).astype(jnp.bfloat16)
        return message_rows(spectra, edge, select, count)
    select = (rows[:, None] == jnp.arange(length_three)[None, :]).astype(jnp.bfloat16)
    chosen = jnp.einsum(
        "rk,jabk->rjba",
        select,
        spectra[:, : half_one + 1],
        preferred_element_type=jnp.float32,
    )
    chosen_edge = jnp.einsum(
        "rk,jak->rja",
        select.astype(jnp.float32),
        edge,
        precision=lax.Precision.HIGHEST,
        preferred_element_type=jnp.float32,
    )
    body = chosen[..., :half_one].reshape(half_px, count, slots * local_two, half_one)
    edge_two = chosen_edge[..., None, :half_one]
    corner = jnp.broadcast_to(chosen_edge[..., None, half_one:], edge_two.shape)
    last = chosen[..., half_one].reshape(half_px, count, slots, local_two)
    edge_one = jnp.stack(
        [
            jnp.pad(
                last[delta],
                (
                    (0, 0),
                    (0, 0),
                    (delta * local_two, (half_px - 1 - delta) * local_two),
                ),
            )
            for delta in range(half_px)
        ]
    )
    edge_one = edge_one.reshape(half_px * count, slots, 1, half_px * local_two)
    edges = jnp.concatenate([edge_two, edge_one, corner], axis=2)
    edges = edges.reshape(half_px, count, 3 * slots, half_one)
    spare = -(slots * (local_two + 3)) % 8
    message = jnp.concatenate([body, edges], axis=2)
    message = jnp.pad(message, ((0, 0), (0, 0), (0, spare), (0, 0)))
    return [message[delta] for delta in range(half_px)]


def on_device(adjoint, saved, spectra, freq_index, picked):
    width_px = lax.axis_size("px")
    width_py = lax.axis_size("py")
    px_index = lax.axis_index("px")
    py_index = lax.axis_index("py")
    devices = width_px * width_py
    half_px = width_px // 2
    half_devices = devices // 2
    half_index = px_index // half_px
    px_low = px_index % half_px
    rows_one, rows_two, length_three = adjoint.shape
    length_one = rows_one * width_px
    length_two = rows_two * width_py
    slots = picked.shape[0]

    order = paired_order(length_three)
    shared_depth = 8
    shared_chunks = SHARED if length_three % (8 * devices * SHARED) == 0 else 0
    shared_count = half_devices * shared_depth
    shared = [
        order[chunk * shared_count : (chunk + 1) * shared_count].reshape(half_devices, -1)
        for chunk in range(shared_chunks)
    ]
    single = order[shared_chunks * shared_count :].reshape(devices, -1)
    depth = single.shape[1]
    owned = [np.concatenate([chunk, chunk]) for chunk in shared] + [single]

    def folded_rows(members):
        folded = np.concatenate(members, axis=1)
        folded = np.minimum(folded, length_three - folded)
        distinct = [list(dict.fromkeys(row.tolist())) for row in folded]
        count = max(len(row) for row in distinct)
        wanted = np.array([row + [row[-1]] * (count - len(row)) for row in distinct])
        places = [[row.index(k) for k in ks] for row, ks in zip(distinct, folded)]
        return wanted, np.array(places)

    half_one = length_one // 2
    edge = lax.ppermute(
        spectra[:, : half_one + 1, 0].astype(jnp.float32),
        "px",
        [(0, half_px), (half_px, 0)],
    )
    last = hartley(length_three)

    def send(value, runs):
        depth = sum(run.shape[1] for run in runs)
        table = left_table(last[np.concatenate([run.reshape(-1) for run in runs])])
        copies = []
        row = 0
        place = 0
        for run in runs:
            for owner in range(run.shape[0]):
                owners = range(owner, devices, run.shape[0])
                planes = [target * depth + place for target in owners]
                copies.append((row, run.shape[1], planes))
                row += run.shape[1]
            place += run.shape[1]
        return forward_last(value, table, devices * depth, copies).reshape(
            devices, depth, rows_one, rows_two
        )

    sent = send(adjoint, shared[:1] + [single])

    def exchange(value):
        return lax.all_to_all(value, ("px", "py"), 0, 0, tiled=True)

    def arranged(value):
        return value.reshape(width_px, width_py, -1, rows_one, rows_two)

    barrier = lax.optimization_barrier
    device = px_index * width_py + py_index
    sent, spectra, edge, adjoint = barrier((sent, spectra, edge, adjoint))
    wanted, places = folded_rows(owned)
    messages = kernel_messages(spectra, edge, wanted, width_px, width_py)
    messages, saved, adjoint, px_index, py_index = barrier(
        (messages, saved, adjoint, px_index, py_index)
    )
    half_index = px_index // half_px
    px_low = px_index % half_px
    messages = send_messages(messages, width_px)
    places = jnp.asarray(places, dtype=jnp.int32)[device]
    local_two = length_two // width_px
    special = (px_low * local_two).astype(jnp.int32).reshape(1)

    order_one = np.arange(length_one // 2)
    order_one = np.concatenate([order_one, (length_one - order_one) % length_one])
    order_one[length_one // 2] = length_one // 2
    slabs = half_index * half_px + (px_low ^ jnp.arange(half_px))
    order_two = (slabs[:, None] * local_two + jnp.arange(local_two)[None, :]).reshape(-1)
    order_two = jnp.concatenate([order_two, partners(order_two, length_two)])
    one = hartley(length_one)[order_one]
    one_f = left_table(one)
    one_b = left_table(one.T)
    sites_two = jnp.arange(length_two)
    two_f = traced_table(sites_two, order_two, length_two, 0)
    two_b = traced_table(order_two, sites_two, length_two, 0)
    sites_half = (slabs[:, None] * rows_one + jnp.arange(rows_one)[None, :]).reshape(-1)
    half_one_b = traced_table(sites_half, jnp.asarray(order_one), length_one, 1)
    near_two = (sites_two + py_index * rows_two) % length_two
    near_two_b = traced_table(order_two, near_two, length_two, 0)
    tables = (one_f, two_f, one_b, two_b)
    half_tables = (one_f, two_f, half_one_b, near_two_b)

    feature_ids = jnp.arange(freq_index.shape[0], dtype=jnp.int32)
    chosen = jnp.sum(
        jnp.where(feature_ids[None, :] == picked[:, None], freq_index[None, :], 0), axis=1
    ).astype(jnp.float32)

    shared_source = (
        (px_low ^ jnp.arange(half_px))[None, :] * width_py
        + ((py_index - jnp.arange(width_py)) % width_py)[:, None]
    ).reshape(-1)

    def shared_fields(index, value):
        first = index * shared_depth
        return filter_planes(
            arranged(value),
            0,
            messages,
            places[first : first + shared_depth],
            special,
            half_tables,
            slots,
            True,
        )

    def shared_rows(pieces):
        return [pieces[0]] + [
            lax.ppermute(pieces[delta], "px", swap_pairs(width_px, half_px, delta))
            for delta in range(1, half_px)
        ]

    def shared_group(index, pieces):
        parts = [jnp.stack([piece[0] for piece in pieces])]
        for shift in range(1, width_py):
            pairs = [(c, (c + shift) % width_py) for c in range(width_py)]
            far = jnp.stack([piece[shift] for piece in pieces])
            parts.append(lax.ppermute(far, "py", pairs))
        return parts, shared_tables[index]

    shared_tables = []
    for chunk in shared:
        ids = jnp.asarray(chunk)[shared_source].reshape(-1)
        shared_tables.append(
            traced_table(ids, jnp.arange(length_three), length_three, 0)
        )
    scale = 1.0 / (length_one * length_two * length_three)
    single_table = right_table(last[single.reshape(-1)])
    first = shared_chunks * shared_depth

    def single_fields(value):
        return filter_planes(
            arranged(value),
            min(first, shared_depth),
            messages,
            places[first:],
            special,
            tables,
            slots,
            False,
        ).reshape(devices, slots, depth, rows_one, rows_two)

    factors = cosine_factors(saved, chosen, scale)
    if shared_chunks == 0:
        returned = exchange(single_fields(exchange(sent)))
        return backward_last([([returned], single_table)], factors, None)

    arrived = exchange(sent)
    sent = send(adjoint, shared[1:])
    sent, messages, places, tables, half_tables, shared_tables, factors = barrier(
        (sent, messages, places, tables, half_tables, shared_tables, factors)
    )
    arrived_late = exchange(sent)
    near = shared_rows(shared_fields(0, arrived))
    fields_single = single_fields(arrived)
    fields_single, near = barrier((fields_single, near))
    returned = exchange(fields_single)
    pieces = shared_fields(1, arrived_late)
    pieces, near = barrier((pieces, near))
    group = shared_group(0, near)
    late = shared_rows(pieces)
    total = backward_last([group], factors, None)
    late, total = barrier((late, total))
    return backward_last(
        [shared_group(1, late), ([returned], single_table)], factors, total
    )


def solution(mesh):
    placed = (
        P(("chain", "px"), "py", None),
        P(("chain", "px"), "py", None),
        P(None, None, "px", None),
        P(),
        P(),
    )
    return jax.shard_map(
        on_device,
        mesh=mesh,
        in_specs=placed,
        out_specs=P(("chain", "px"), "py", None),
        check_vma=False,
    )
```

```python
import math

import jax
import jax.numpy as jnp
import numpy as np
from jax import lax
from jax.experimental import pallas as pl
from jax.experimental.pallas import tpu as pltpu
from jax.sharding import PartitionSpec as P

VMEM_BYTES = 56 * 1024 * 1024
LAST_BYTES = 48 * 1024 * 1024
SHARED = 2
GROUP = 4


def hartley(length):
    counter = np.arange(length)
    angle = 2.0 * np.pi * ((counter[:, None] * counter[None, :]) % length) / length
    return np.cos(angle) + np.sin(angle)


def split_table(table):
    high = table.astype(np.float32).astype(jnp.bfloat16)
    low = (table - high.astype(np.float64)).astype(np.float32).astype(jnp.bfloat16)
    return high, low


def left_table(table):
    high, low = split_table(table)
    return jnp.asarray(np.concatenate([high, high, low], axis=1))


def right_table(table):
    high, low = split_table(table)
    return jnp.asarray(np.concatenate([high, high, low], axis=0))


def traced_table(rows, columns, length, axis):
    product = rows[:, None] * columns[None, :] % length
    angle = product.astype(jnp.float32) * (2.0 * math.pi / length)
    value = jnp.cos(angle) + jnp.sin(angle)
    high = lax.reduce_precision(value, 8, 7)
    low = value - high
    return jnp.concatenate([high, high, low], axis=axis).astype(jnp.bfloat16)


def partners(first, length):
    base = first % (length // 2) == 0
    return jnp.where(base, (first + length // 2) % length, (length - first) % length)


def paired_order(length):
    half = length // 2
    order = [0, half]
    for index in range(1, half):
        order += [index, length - index]
    return np.array(order)


def split_value(value):
    high = value.astype(jnp.bfloat16)
    low = (value - high.astype(jnp.float32)).astype(jnp.bfloat16)
    return high, low


def left_dot(table, value):
    high, low = split_value(value)
    stacked = jnp.concatenate([high, low, high], axis=0)
    return jnp.dot(table, stacked, preferred_element_type=jnp.float32)


def right_dot(value, table):
    high, low = split_value(value)
    stacked = jnp.concatenate([high, low, high], axis=1)
    return jnp.dot(stacked, table, preferred_element_type=jnp.float32)


def params(limit=VMEM_BYTES):
    return pltpu.CompilerParams(vmem_limit_bytes=limit)


def forward_last(adjoint, table, depth, copies):
    rows_one, rows_two, length = adjoint.shape
    count = table.shape[0]
    block = min(16, rows_one)

    def body(adjoint_ref, table_ref, out_ref):
        flat = out_ref.reshape(depth * block, rows_two)
        for start in range(0, block, 2):
            value = adjoint_ref[start : start + 2].reshape(2 * rows_two, length)
            high, low = split_value(value)
            stacked = jnp.concatenate([high, low, high], axis=1)
            result = lax.dot_general(
                table_ref[...],
                stacked,
                (((1,), (1,)), ((), ())),
                preferred_element_type=jnp.float32,
            )
            for inner in range(2):
                columns = slice(inner * rows_two, (inner + 1) * rows_two)
                for row, rows, planes in copies:
                    for plane in planes:
                        flat[
                            pl.ds(plane * block + start + inner, rows, stride=block), :
                        ] = result[row : row + rows, columns]

    return pl.pallas_call(
        body,
        grid=(rows_one // block,),
        in_specs=[
            pl.BlockSpec((block, rows_two, length), lambda i: (i, 0, 0)),
            pl.BlockSpec(table.shape, lambda i: (0, 0)),
        ],
        out_specs=pl.BlockSpec((depth, block, rows_two), lambda i: (0, i, 0)),
        out_shape=jax.ShapeDtypeStruct((depth, rows_one, rows_two), jnp.float32),
        compiler_params=params(),
        cost_estimate=pl.CostEstimate(
            flops=6 * count * rows_one * rows_two * length,
            bytes_accessed=4 * rows_one * rows_two * (length + depth),
            transcendentals=0,
        ),
        name="forward_last",
    )(adjoint, table)


def whole_plane(message_refs, slot, slots, special, local_two):
    blocks = [ref[0] for ref in message_refs]
    body = [block[slot * local_two : (slot + 1) * local_two] for block in blocks]
    folded = jnp.concatenate(body, axis=0)
    first = slots * local_two + 3 * slot
    edges = blocks[0][first : first + 3]
    for block in blocks[1:]:
        edges = edges + block[first : first + 3]
    edge_two, edge_one, corner = edges[0:1], edges[1:2], edges[2:3]
    extent = folded.shape
    row = lax.broadcasted_iota(jnp.int32, extent, 0)
    column = lax.broadcasted_iota(jnp.int32, extent, 1)
    right = jnp.where(row == special, edge_two, folded).T
    left = folded.T
    top = row == 0
    lower_left = jnp.where(top, edge_one, left)
    lower_right = jnp.where(top, jnp.where(column == special, corner, edge_one), right)
    return jnp.concatenate(
        [
            jnp.concatenate([left, right], axis=1),
            jnp.concatenate([lower_left, lower_right], axis=1),
        ],
        axis=0,
    )


def filter_planes(planes, first, messages, places, special, tables, slots, split):
    width_px, width_py, _, rows_one, rows_two = planes.shape
    planes_count = places.shape[0]
    length_one = width_px * rows_one
    length_two = width_py * rows_two
    out_px = tables[2].shape[0] // rows_one
    message_rows = messages[0].shape[1]
    local_two = length_two // 2 // len(messages)
    group = next(g for g in (GROUP, 2, 1) if planes_count % g == 0 and first % g == 0)

    def body(places_ref, special_ref, planes_ref, *refs):
        one_f, two_f, one_b, two_b = refs[group * len(messages) :][:4]
        out_refs = refs[group * len(messages) + 4 :]
        values = []
        for member in range(group):
            value = jnp.concatenate(
                [
                    planes_ref[:, part, member].reshape(length_one, rows_two)
                    for part in range(width_py)
                ],
                axis=1,
            )
            values.append(right_dot(value, two_f[...]))
        values = [left_dot(one_f[...], value) for value in values]
        for slot in range(slots):
            backs = []
            for member, value in enumerate(values):
                message_refs = refs[member * len(messages) : (member + 1) * len(messages)]
                plane = whole_plane(message_refs, slot, slots, special_ref[0], local_two)
                backs.append(left_dot(one_b[...], value * plane))
            for member, back in enumerate(backs):
                back = right_dot(back, two_b[...])
                for part in range(width_py):
                    piece = back[:, part * rows_two : (part + 1) * rows_two]
                    if split:
                        for index in range(out_px):
                            out_refs[index][part, slot, member] = piece[
                                index * rows_one : (index + 1) * rows_one
                            ]
                    else:
                        out_refs[0][:, part, slot, member] = piece.reshape(
                            out_px, rows_one, rows_two
                        )

    plane_size = length_one * length_two
    if split:
        extent = (width_py, slots, planes_count, rows_one, rows_two)
        out_shape = [jax.ShapeDtypeStruct(extent, jnp.float32)] * out_px
        out_specs = [
            pl.BlockSpec(
                (width_py, slots, group, rows_one, rows_two),
                lambda i, *_: (0, 0, i, 0, 0),
            )
        ] * out_px
    else:
        extent = (out_px, width_py, slots, planes_count, rows_one, rows_two)
        out_shape = [jax.ShapeDtypeStruct(extent, jnp.float32)]
        out_specs = [
            pl.BlockSpec(
                (out_px, width_py, slots, group, rows_one, rows_two),
                lambda i, *_: (0, 0, 0, i, 0, 0),
            )
        ]

    def message_spec(member):
        return pl.BlockSpec(
            (1, message_rows, length_one // 2),
            lambda i, places_ref, special_ref: (places_ref[group * i + member], 0, 0),
        )

    out_rows = out_px * rows_one
    outs = pl.pallas_call(
        body,
        grid_spec=pltpu.PrefetchScalarGridSpec(
            num_scalar_prefetch=2,
            grid=(planes_count // group,),
            in_specs=[
                pl.BlockSpec(
                    (width_px, width_py, group, rows_one, rows_two),
                    lambda i, *_: (0, 0, first // group + i, 0, 0),
                )
            ]
            + [message_spec(member) for member in range(group) for _ in messages]
            + [pl.BlockSpec(table.shape, lambda i, *_: (0, 0)) for table in tables],
            out_specs=out_specs,
        ),
        out_shape=out_shape,
        compiler_params=params(),
        cost_estimate=pl.CostEstimate(
            flops=6
            * planes_count
            * (
                plane_size * (length_one + length_two)
                + slots * out_rows * length_two * (length_one + length_two)
            ),
            bytes_accessed=4
            * planes_count
            * (plane_size + slots * (plane_size // 4 + out_rows * length_two)),
            transcendentals=0,
        ),
        name="filter_planes",
    )(places, special, planes, *(messages * group), *tables)
    return outs if split else outs[0]


def backward_last(groups, factors, total):
    parts = [part for members, _ in groups for part in members]
    tables = [table for _, table in groups]
    slots = factors.shape[0]
    rows_one, rows_two = parts[0].shape[3:]
    length = tables[0].shape[1]
    block = min(8, rows_one)

    def body(*refs):
        factors_ref = refs[0]
        table_refs = refs[1 : 1 + len(groups)]
        part_refs = refs[1 + len(groups) : 1 + len(groups) + len(parts)]
        out_ref = refs[-1]
        flats = [
            ref.reshape(math.prod(part.shape[:3]) * block, rows_two)
            for ref, part in zip(part_refs, parts)
        ]

        def columns(slot, site, first, last):
            found = []
            for index in range(first, last):
                sources, _, depth = parts[index].shape[:3]
                for source in range(sources):
                    row = (source * slots + slot) * depth * block + site
                    found.append(flats[index][pl.ds(row, depth, stride=block), :])
            value = jnp.concatenate(found, axis=0)
            if value.shape[0] * 2 != rows_two:
                return value.T
            high = value.astype(jnp.bfloat16).astype(jnp.float32)
            return jnp.concatenate([high, value - high], axis=0).T

        for start in range(0, block, 2):
            result = None
            for slot in range(slots):
                field = None
                first = 0
                for (members, _), table_ref in zip(groups, table_refs):
                    last = first + len(members)
                    value = jnp.concatenate(
                        [columns(slot, start + inner, first, last) for inner in range(2)],
                        axis=0,
                    )
                    if value.shape[1] * 3 == table_ref.shape[0]:
                        value = right_dot(value, table_ref[...])
                    else:
                        value = value.astype(jnp.bfloat16)
                        value = jnp.dot(
                            jnp.concatenate([value, value], axis=1),
                            jnp.concatenate(
                                [table_ref[...], jnp.zeros_like(table_ref[: value.shape[1] // 2])],
                                axis=0,
                            ),
                            preferred_element_type=jnp.float32,
                        )
                    field = value if field is None else field + value
                    first = last
                field = field.reshape(2, rows_two, length)
                term = field * factors_ref[slot, start : start + 2]
                result = term if result is None else result + term
            if total is not None:
                result = result + refs[-2][start : start + 2]
            out_ref[start : start + 2] = result

    space = pl.BlockSpec((block, rows_two, length), lambda i: (i, 0, 0))
    operands = [factors] + tables + parts
    in_specs = (
        [pl.BlockSpec((slots, block, rows_two, length), lambda i: (0, i, 0, 0))]
        + [pl.BlockSpec(table.shape, lambda i: (0, 0)) for table in tables]
        + [
            pl.BlockSpec(part.shape[:3] + (block, rows_two), lambda i: (0, 0, 0, i, 0))
            for part in parts
        ]
    )
    if total is not None:
        operands.append(total)
        in_specs.append(space)
    size = rows_one * rows_two
    planes_count = sum(part.shape[0] * part.shape[2] for part in parts)
    return pl.pallas_call(
        body,
        grid=(rows_one // block,),
        in_specs=in_specs,
        out_specs=space,
        out_shape=jax.ShapeDtypeStruct((rows_one, rows_two, length), jnp.float32),
        compiler_params=params(LAST_BYTES),
        cost_estimate=pl.CostEstimate(
            flops=6 * slots * size * planes_count * length,
            bytes_accessed=4 * size * (slots * planes_count + (2 + slots) * length),
            transcendentals=0,
        ),
        name="backward_last",
    )(*operands)


def cosine_turns():
    points = np.cos(np.pi * (np.arange(64) + 0.5) / 64) * 0.125 + 0.125
    fit = np.polynomial.Polynomial.fit(
        points, np.cos(2.0 * np.pi * np.sqrt(points)), 8, domain=[0.0, 0.25]
    )
    return [float(value) for value in fit.convert().coef]


def cosine_factors(saved, chosen, scale):
    rows_one, rows_two, length = saved.shape
    slots = chosen.shape[0]
    block = min(8, rows_one)
    coefficients = cosine_turns()

    def body(chosen_ref, saved_ref, out_ref):
        for slot in range(slots):
            feature = chosen_ref[slot]
            turns = saved_ref[...] * (feature * (1.0 / 16.0))
            turns = turns - jnp.round(turns)
            square = turns * turns
            result = jnp.full_like(square, coefficients[-1])
            for value in coefficients[-2::-1]:
                result = result * square + value
            out_ref[slot] = result * (feature * (math.pi / 8.0 * scale))

    size = rows_one * rows_two * length
    return pl.pallas_call(
        body,
        grid=(rows_one // block,),
        in_specs=[
            pl.BlockSpec(memory_space=pltpu.SMEM),
            pl.BlockSpec((block, rows_two, length), lambda i: (i, 0, 0)),
        ],
        out_specs=pl.BlockSpec((slots, block, rows_two, length), lambda i: (0, i, 0, 0)),
        out_shape=jax.ShapeDtypeStruct((slots, rows_one, rows_two, length), jnp.float32),
        compiler_params=params(),
        cost_estimate=pl.CostEstimate(
            flops=24 * slots * size, bytes_accessed=4 * size * (1 + slots), transcendentals=0
        ),
        name="cosine_factors",
    )(chosen, saved)


def swap_pairs(width_px, half_px, delta):
    return [(px, px // half_px * half_px + (px % half_px ^ delta)) for px in range(width_px)]


def send_messages(message, width_px):
    half_px = width_px // 2
    if half_px <= 8:
        return [message[0]] + [
            lax.ppermute(message[delta], "px", swap_pairs(width_px, half_px, delta))
            for delta in range(1, half_px)
        ]
    groups = [list(range(half_px)), list(range(half_px, width_px))]
    index = lax.axis_index("px") % half_px ^ jnp.arange(half_px)
    message = jnp.take(jnp.stack(message), index, axis=0)
    message = lax.all_to_all(message, "px", 0, 0, axis_index_groups=groups, tiled=True)
    message = jnp.take(message, index, axis=0)
    return [message[delta] for delta in range(half_px)]


def message_rows(spectra, edge, select, count):
    slots, length_one, local_two, length_three = spectra.shape
    half_one = length_one // 2
    half_px = half_one // local_two
    padded = select.shape[0] // half_px
    used = slots * (local_two + 3)
    extent = used + -used % 8
    group = 4
    lanes = 128

    def body(spectra_ref, edge_ref, select_ref, *refs):
        flats = [ref.reshape(count * extent, half_one) for ref in refs[:half_px]]
        scratch = refs[half_px:]

        def chosen(value):
            return lax.dot_general(
                select_ref[...],
                value.astype(jnp.bfloat16),
                (((1,), (1,)), ((), ())),
                preferred_element_type=jnp.float32,
            )

        def store(value, row):
            for delta in range(half_px):
                flats[delta][pl.ds(row, count, stride=extent), :] = value[
                    delta * padded : delta * padded + count
                ]

        for slot in range(slots):
            for part, ref in enumerate(scratch):
                ref[...] = (
                    spectra_ref[slot, :half_one, :, part * lanes : (part + 1) * lanes]
                    .astype(jnp.float32)
                    .reshape(half_one * local_two, lanes)
                )
            for start in range(0, local_two, group):
                value = jnp.concatenate(
                    [
                        jnp.concatenate(
                            [
                                ref[pl.ds(start + inner, half_one, stride=local_two), :]
                                for ref in scratch
                            ],
                            axis=1,
                        )
                        for inner in range(group)
                    ],
                    axis=0,
                )
                value = chosen(value)
                for inner in range(group):
                    store(
                        value[:, inner * half_one : (inner + 1) * half_one],
                        slot * local_two + start + inner,
                    )
            first = slots * local_two + 3 * slot
            store(chosen(edge_ref[slot, :half_one]), first)
            tiled = jnp.concatenate([spectra_ref[slot, half_one]] * half_px, axis=0)
            value = chosen(tiled)
            row = lax.broadcasted_iota(jnp.int32, value.shape, 0) // padded
            lane = lax.broadcasted_iota(jnp.int32, value.shape, 1) // local_two
            store(jnp.where(row == lane, value, 0.0), first + 1)
            corner = edge_ref[slot, half_one : half_one + 1]
            store(chosen(jnp.broadcast_to(corner, (half_one, length_three))), first + 2)
        for flat in flats:
            for row in range(used, extent):
                flat[pl.ds(row, count, stride=extent), :] = jnp.zeros(
                    (count, half_one), jnp.float32
                )

    part = (slots, half_one + 1, local_two, length_three)
    return pl.pallas_call(
        body,
        grid=(1,),
        in_specs=[
            pl.BlockSpec(part, lambda i: (0, 0, 0, 0)),
            pl.BlockSpec(edge.shape, lambda i: (0, 0, 0)),
            pl.BlockSpec(select.shape, lambda i: (0, 0)),
        ],
        out_specs=[pl.BlockSpec((count, extent, half_one), lambda i: (0, 0, 0))] * half_px,
        out_shape=[jax.ShapeDtypeStruct((count, extent, half_one), jnp.float32)] * half_px,
        scratch_shapes=[pltpu.VMEM((half_one * local_two, lanes), jnp.float32)]
        * (length_three // lanes),
        compiler_params=params(),
        cost_estimate=pl.CostEstimate(
            flops=2 * slots * select.shape[0] * half_one * local_two * length_three,
            bytes_accessed=2 * math.prod(part) + 4 * half_px * count * extent * half_one,
            transcendentals=0,
        ),
        name="message_rows",
    )(spectra, edge, select)


def kernel_messages(spectra, edge, wanted, width_px, width_py):
    slots, length_one, local_two, length_three = spectra.shape
    half_one = length_one // 2
    half_px = width_px // 2
    count = wanted.shape[1]
    px_index = lax.axis_index("px")
    py_index = lax.axis_index("py")
    wanted = wanted.reshape(width_px, width_py, count)
    sources = np.arange(width_px)
    targets = np.stack(
        [sources // half_px * half_px + (sources % half_px ^ d) for d in range(half_px)],
        axis=1,
    )
    rows = jnp.asarray(wanted[targets].transpose(0, 2, 1, 3).reshape(-1, half_px * count))
    rows = rows[px_index * width_py + py_index]
    sublanes = 16
    if local_two % sublanes == 0:
        padded = count + -count % sublanes
        rows = rows.reshape(half_px, count)
        rows = jnp.pad(rows, ((0, 0), (0, padded - count)), constant_values=-1)
        rows = rows.reshape(-1)
        select = (rows[:, None] == jnp.arange(length_three)[None, :]).astype(jnp.bfloat16)
        return message_rows(spectra, edge, select, count)
    select = (rows[:, None] == jnp.arange(length_three)[None, :]).astype(jnp.bfloat16)
    chosen = jnp.einsum(
        "rk,jabk->rjba",
        select,
        spectra[:, : half_one + 1],
        preferred_element_type=jnp.float32,
    )
    chosen_edge = jnp.einsum(
        "rk,jak->rja",
        select.astype(jnp.float32),
        edge,
        precision=lax.Precision.HIGHEST,
        preferred_element_type=jnp.float32,
    )
    body = chosen[..., :half_one].reshape(half_px, count, slots * local_two, half_one)
    edge_two = chosen_edge[..., None, :half_one]
    corner = jnp.broadcast_to(chosen_edge[..., None, half_one:], edge_two.shape)
    last = chosen[..., half_one].reshape(half_px, count, slots, local_two)
    edge_one = jnp.stack(
        [
            jnp.pad(
                last[delta],
                (
                    (0, 0),
                    (0, 0),
                    (delta * local_two, (half_px - 1 - delta) * local_two),
                ),
            )
            for delta in range(half_px)
        ]
    )
    edge_one = edge_one.reshape(half_px * count, slots, 1, half_px * local_two)
    edges = jnp.concatenate([edge_two, edge_one, corner], axis=2)
    edges = edges.reshape(half_px, count, 3 * slots, half_one)
    spare = -(slots * (local_two + 3)) % 8
    message = jnp.concatenate([body, edges], axis=2)
    message = jnp.pad(message, ((0, 0), (0, 0), (0, spare), (0, 0)))
    return [message[delta] for delta in range(half_px)]


def on_device(adjoint, saved, spectra, freq_index, picked):
    width_px = lax.axis_size("px")
    width_py = lax.axis_size("py")
    px_index = lax.axis_index("px")
    py_index = lax.axis_index("py")
    devices = width_px * width_py
    half_px = width_px // 2
    half_devices = devices // 2
    half_index = px_index // half_px
    px_low = px_index % half_px
    rows_one, rows_two, length_three = adjoint.shape
    length_one = rows_one * width_px
    length_two = rows_two * width_py
    slots = picked.shape[0]

    order = paired_order(length_three)
    shared_depth = 8
    shared_chunks = SHARED if length_three % (8 * devices * SHARED) == 0 else 0
    shared_count = half_devices * shared_depth
    shared = [
        order[chunk * shared_count : (chunk + 1) * shared_count].reshape(half_devices, -1)
        for chunk in range(shared_chunks)
    ]
    single = order[shared_chunks * shared_count :].reshape(devices, -1)
    depth = single.shape[1]
    owned = [np.concatenate([chunk, chunk]) for chunk in shared] + [single]

    def folded_rows(members):
        folded = np.concatenate(members, axis=1)
        folded = np.minimum(folded, length_three - folded)
        distinct = [list(dict.fromkeys(row.tolist())) for row in folded]
        count = max(len(row) for row in distinct)
        wanted = np.array([row + [row[-1]] * (count - len(row)) for row in distinct])
        places = [[row.index(k) for k in ks] for row, ks in zip(distinct, folded)]
        return wanted, np.array(places)

    half_one = length_one // 2
    edge = lax.ppermute(
        spectra[:, : half_one + 1, 0].astype(jnp.float32),
        "px",
        [(0, half_px), (half_px, 0)],
    )
    last = hartley(length_three)

    def send(value, runs):
        depth = sum(run.shape[1] for run in runs)
        table = left_table(last[np.concatenate([run.reshape(-1) for run in runs])])
        copies = []
        row = 0
        place = 0
        for run in runs:
            for owner in range(run.shape[0]):
                owners = range(owner, devices, run.shape[0])
                planes = [target * depth + place for target in owners]
                copies.append((row, run.shape[1], planes))
                row += run.shape[1]
            place += run.shape[1]
        return forward_last(value, table, devices * depth, copies).reshape(
            devices, depth, rows_one, rows_two
        )

    sent = send(adjoint, shared[:1] + [single])

    def exchange(value):
        return lax.all_to_all(value, ("px", "py"), 0, 0, tiled=True)

    def arranged(value):
        return value.reshape(width_px, width_py, -1, rows_one, rows_two)

    barrier = lax.optimization_barrier
    device = px_index * width_py + py_index
    sent, spectra, _, adjoint = barrier((sent, spectra, edge[0, 0, :1], adjoint))
    wanted, places = folded_rows(owned)
    messages = kernel_messages(spectra, edge, wanted, width_px, width_py)
    messages, saved, adjoint, px_index, py_index = barrier(
        (messages, saved, adjoint, px_index, py_index)
    )
    half_index = px_index // half_px
    px_low = px_index % half_px
    messages = send_messages(messages, width_px)
    places = jnp.asarray(places, dtype=jnp.int32)[device]
    local_two = length_two // width_px
    special = (px_low * local_two).astype(jnp.int32).reshape(1)

    order_one = np.arange(length_one // 2)
    order_one = np.concatenate([order_one, (length_one - order_one) % length_one])
    order_one[length_one // 2] = length_one // 2
    slabs = half_index * half_px + (px_low ^ jnp.arange(half_px))
    order_two = (slabs[:, None] * local_two + jnp.arange(local_two)[None, :]).reshape(-1)
    order_two = jnp.concatenate([order_two, partners(order_two, length_two)])
    one = hartley(length_one)[order_one]
    one_f = left_table(one)
    one_b = left_table(one.T)
    sites_two = jnp.arange(length_two)
    two_f = traced_table(sites_two, order_two, length_two, 0)
    two_b = traced_table(order_two, sites_two, length_two, 0)
    sites_half = (slabs[:, None] * rows_one + jnp.arange(rows_one)[None, :]).reshape(-1)
    half_one_b = traced_table(sites_half, jnp.asarray(order_one), length_one, 1)
    near_two = (sites_two + py_index * rows_two) % length_two
    near_two_b = traced_table(order_two, near_two, length_two, 0)
    tables = (one_f, two_f, one_b, two_b)
    half_tables = (one_f, two_f, half_one_b, near_two_b)

    feature_ids = jnp.arange(freq_index.shape[0], dtype=jnp.int32)
    chosen = jnp.sum(
        jnp.where(feature_ids[None, :] == picked[:, None], freq_index[None, :], 0), axis=1
    ).astype(jnp.float32)

    shared_source = (
        (px_low ^ jnp.arange(half_px))[None, :] * width_py
        + ((py_index - jnp.arange(width_py)) % width_py)[:, None]
    ).reshape(-1)

    def shared_fields(index, value):
        first = index * shared_depth
        return filter_planes(
            arranged(value),
            0,
            messages,
            places[first : first + shared_depth],
            special,
            half_tables,
            slots,
            True,
        )

    def shared_rows(pieces):
        return [pieces[0]] + [
            lax.ppermute(pieces[delta], "px", swap_pairs(width_px, half_px, delta))
            for delta in range(1, half_px)
        ]

    def shared_group(index, pieces):
        parts = [jnp.stack([piece[0] for piece in pieces])]
        for shift in range(1, width_py):
            pairs = [(c, (c + shift) % width_py) for c in range(width_py)]
            far = jnp.stack([piece[shift] for piece in pieces])
            parts.append(lax.ppermute(far, "py", pairs))
        return parts, shared_tables[index]

    shared_tables = []
    for chunk in shared:
        ids = jnp.asarray(chunk)[shared_source].reshape(-1)
        shared_tables.append(
            traced_table(ids, jnp.arange(length_three), length_three, 0)
        )
    scale = 1.0 / (length_one * length_two * length_three)
    single_table = right_table(last[single.reshape(-1)])
    first = shared_chunks * shared_depth

    def single_fields(value):
        return filter_planes(
            arranged(value),
            min(first, shared_depth),
            messages,
            places[first:],
            special,
            tables,
            slots,
            False,
        ).reshape(devices, slots, depth, rows_one, rows_two)

    factors = cosine_factors(saved, chosen, scale)
    if shared_chunks == 0:
        returned = exchange(single_fields(exchange(sent)))
        return backward_last([([returned], single_table)], factors, None)

    arrived = exchange(sent)
    sent = send(adjoint, shared[1:])
    sent, messages, places, tables, half_tables, shared_tables, factors = barrier(
        (sent, messages, places, tables, half_tables, shared_tables, factors)
    )
    arrived_late = exchange(sent)
    near = shared_rows(shared_fields(0, arrived))
    fields_single = single_fields(arrived)
    fields_single, near = barrier((fields_single, near))
    returned = exchange(fields_single)
    pieces = shared_fields(1, arrived_late)
    pieces, near = barrier((pieces, near))
    group = shared_group(0, near)
    late = shared_rows(pieces)
    total = backward_last([group], factors, None)
    late, total = barrier((late, total))
    return backward_last(
        [shared_group(1, late), ([returned], single_table)], factors, total
    )


def solution(mesh):
    placed = (
        P(("chain", "px"), "py", None),
        P(("chain", "px"), "py", None),
        P(None, None, "px", None),
        P(),
        P(),
    )
    return jax.shard_map(
        on_device,
        mesh=mesh,
        in_specs=placed,
        out_specs=P(("chain", "px"), "py", None),
        check_vma=False,
    )
```

```python
import math

import jax
import jax.numpy as jnp
import numpy as np
from jax import lax
from jax.experimental import pallas as pl
from jax.experimental.pallas import tpu as pltpu
from jax.sharding import PartitionSpec as P

VMEM_BYTES = 56 * 1024 * 1024
LAST_BYTES = 48 * 1024 * 1024
SHARED = 2
GROUP = 4


def hartley(length):
    counter = np.arange(length)
    angle = 2.0 * np.pi * ((counter[:, None] * counter[None, :]) % length) / length
    return np.cos(angle) + np.sin(angle)


def split_table(table):
    high = table.astype(np.float32).astype(jnp.bfloat16)
    low = (table - high.astype(np.float64)).astype(np.float32).astype(jnp.bfloat16)
    return high, low


def left_table(table):
    high, low = split_table(table)
    return jnp.asarray(np.concatenate([high, high, low], axis=1))


def right_table(table):
    high, low = split_table(table)
    return jnp.asarray(np.concatenate([high, high, low], axis=0))


def traced_table(rows, columns, length, axis):
    product = rows[:, None] * columns[None, :] % length
    angle = product.astype(jnp.float32) * (2.0 * math.pi / length)
    value = jnp.cos(angle) + jnp.sin(angle)
    high = lax.reduce_precision(value, 8, 7)
    low = value - high
    return jnp.concatenate([high, high, low], axis=axis).astype(jnp.bfloat16)


def partners(first, length):
    base = first % (length // 2) == 0
    return jnp.where(base, (first + length // 2) % length, (length - first) % length)


def paired_order(length):
    half = length // 2
    order = [0, half]
    for index in range(1, half):
        order += [index, length - index]
    return np.array(order)


def split_value(value):
    high = value.astype(jnp.bfloat16)
    low = (value - high.astype(jnp.float32)).astype(jnp.bfloat16)
    return high, low


def left_dot(table, value):
    high, low = split_value(value)
    stacked = jnp.concatenate([high, low, high], axis=0)
    return jnp.dot(table, stacked, preferred_element_type=jnp.float32)


def right_dot(value, table):
    high, low = split_value(value)
    stacked = jnp.concatenate([high, low, high], axis=1)
    return jnp.dot(stacked, table, preferred_element_type=jnp.float32)


def params(limit=VMEM_BYTES):
    return pltpu.CompilerParams(vmem_limit_bytes=limit)


def forward_last(adjoint, table, depth, copies):
    rows_one, rows_two, length = adjoint.shape
    count = table.shape[0]
    block = min(16, rows_one)

    def body(adjoint_ref, table_ref, out_ref):
        flat = out_ref.reshape(depth * block, rows_two)
        for start in range(0, block, 2):
            value = adjoint_ref[start : start + 2].reshape(2 * rows_two, length)
            high, low = split_value(value)
            stacked = jnp.concatenate([high, low, high], axis=1)
            result = lax.dot_general(
                table_ref[...],
                stacked,
                (((1,), (1,)), ((), ())),
                preferred_element_type=jnp.float32,
            )
            for inner in range(2):
                columns = slice(inner * rows_two, (inner + 1) * rows_two)
                for row, rows, planes in copies:
                    for plane in planes:
                        flat[
                            pl.ds(plane * block + start + inner, rows, stride=block), :
                        ] = result[row : row + rows, columns]

    return pl.pallas_call(
        body,
        grid=(rows_one // block,),
        in_specs=[
            pl.BlockSpec((block, rows_two, length), lambda i: (i, 0, 0)),
            pl.BlockSpec(table.shape, lambda i: (0, 0)),
        ],
        out_specs=pl.BlockSpec((depth, block, rows_two), lambda i: (0, i, 0)),
        out_shape=jax.ShapeDtypeStruct((depth, rows_one, rows_two), jnp.float32),
        compiler_params=params(),
        cost_estimate=pl.CostEstimate(
            flops=6 * count * rows_one * rows_two * length,
            bytes_accessed=4 * rows_one * rows_two * (length + depth),
            transcendentals=0,
        ),
        name="forward_last",
    )(adjoint, table)


def whole_plane(message_refs, slot, slots, special, local_two):
    blocks = [ref[0] for ref in message_refs]
    body = [block[slot * local_two : (slot + 1) * local_two] for block in blocks]
    folded = jnp.concatenate(body, axis=0)
    first = slots * local_two + 3 * slot
    edges = blocks[0][first : first + 3]
    for block in blocks[1:]:
        edges = edges + block[first : first + 3]
    edge_two, edge_one, corner = edges[0:1], edges[1:2], edges[2:3]
    extent = folded.shape
    row = lax.broadcasted_iota(jnp.int32, extent, 0)
    column = lax.broadcasted_iota(jnp.int32, extent, 1)
    right = jnp.where(row == special, edge_two, folded).T
    left = folded.T
    top = row == 0
    lower_left = jnp.where(top, edge_one, left)
    lower_right = jnp.where(top, jnp.where(column == special, corner, edge_one), right)
    return jnp.concatenate(
        [
            jnp.concatenate([left, right], axis=1),
            jnp.concatenate([lower_left, lower_right], axis=1),
        ],
        axis=0,
    )


def filter_planes(planes, first, messages, places, special, tables, slots, split):
    width_px, width_py, _, rows_one, rows_two = planes.shape
    planes_count = places.shape[0]
    length_one = width_px * rows_one
    length_two = width_py * rows_two
    out_px = tables[2].shape[0] // rows_one
    message_rows = messages[0].shape[1]
    local_two = length_two // 2 // len(messages)
    group = next(g for g in (GROUP, 2, 1) if planes_count % g == 0 and first % g == 0)

    def body(places_ref, special_ref, planes_ref, *refs):
        one_f, two_f, one_b, two_b = refs[group * len(messages) :][:4]
        out_refs = refs[group * len(messages) + 4 :]
        values = []
        for member in range(group):
            value = jnp.concatenate(
                [
                    planes_ref[:, part, member].reshape(length_one, rows_two)
                    for part in range(width_py)
                ],
                axis=1,
            )
            values.append(right_dot(value, two_f[...]))
        values = [left_dot(one_f[...], value) for value in values]
        for slot in range(slots):
            backs = []
            for member, value in enumerate(values):
                message_refs = refs[member * len(messages) : (member + 1) * len(messages)]
                plane = whole_plane(message_refs, slot, slots, special_ref[0], local_two)
                backs.append(left_dot(one_b[...], value * plane))
            for member, back in enumerate(backs):
                back = right_dot(back, two_b[...])
                for part in range(width_py):
                    piece = back[:, part * rows_two : (part + 1) * rows_two]
                    if split:
                        for index in range(out_px):
                            out_refs[index][part, slot, member] = piece[
                                index * rows_one : (index + 1) * rows_one
                            ]
                    else:
                        out_refs[0][:, part, slot, member] = piece.reshape(
                            out_px, rows_one, rows_two
                        )

    plane_size = length_one * length_two
    if split:
        extent = (width_py, slots, planes_count, rows_one, rows_two)
        out_shape = [jax.ShapeDtypeStruct(extent, jnp.float32)] * out_px
        out_specs = [
            pl.BlockSpec(
                (width_py, slots, group, rows_one, rows_two),
                lambda i, *_: (0, 0, i, 0, 0),
            )
        ] * out_px
    else:
        extent = (out_px, width_py, slots, planes_count, rows_one, rows_two)
        out_shape = [jax.ShapeDtypeStruct(extent, jnp.float32)]
        out_specs = [
            pl.BlockSpec(
                (out_px, width_py, slots, group, rows_one, rows_two),
                lambda i, *_: (0, 0, 0, i, 0, 0),
            )
        ]

    def message_spec(member):
        return pl.BlockSpec(
            (1, message_rows, length_one // 2),
            lambda i, places_ref, special_ref: (places_ref[group * i + member], 0, 0),
        )

    out_rows = out_px * rows_one
    outs = pl.pallas_call(
        body,
        grid_spec=pltpu.PrefetchScalarGridSpec(
            num_scalar_prefetch=2,
            grid=(planes_count // group,),
            in_specs=[
                pl.BlockSpec(
                    (width_px, width_py, group, rows_one, rows_two),
                    lambda i, *_: (0, 0, first // group + i, 0, 0),
                )
            ]
            + [message_spec(member) for member in range(group) for _ in messages]
            + [pl.BlockSpec(table.shape, lambda i, *_: (0, 0)) for table in tables],
            out_specs=out_specs,
        ),
        out_shape=out_shape,
        compiler_params=params(),
        cost_estimate=pl.CostEstimate(
            flops=6
            * planes_count
            * (
                plane_size * (length_one + length_two)
                + slots * out_rows * length_two * (length_one + length_two)
            ),
            bytes_accessed=4
            * planes_count
            * (plane_size + slots * (plane_size // 4 + out_rows * length_two)),
            transcendentals=0,
        ),
        name="filter_planes",
    )(places, special, planes, *(messages * group), *tables)
    return outs if split else outs[0]


def backward_last(groups, factors, total):
    parts = [part for members, _ in groups for part in members]
    tables = [table for _, table in groups]
    slots = factors.shape[0]
    rows_one, rows_two = parts[0].shape[3:]
    length = tables[0].shape[1]
    block = min(8, rows_one)

    def body(*refs):
        factors_ref = refs[0]
        table_refs = refs[1 : 1 + len(groups)]
        part_refs = refs[1 + len(groups) : 1 + len(groups) + len(parts)]
        out_ref = refs[-1]
        flats = [
            ref.reshape(math.prod(part.shape[:3]) * block, rows_two)
            for ref, part in zip(part_refs, parts)
        ]

        def columns(slot, site, first, last):
            found = []
            for index in range(first, last):
                sources, _, depth = parts[index].shape[:3]
                for source in range(sources):
                    row = (source * slots + slot) * depth * block + site
                    found.append(flats[index][pl.ds(row, depth, stride=block), :])
            value = jnp.concatenate(found, axis=0)
            if value.shape[0] * 2 != rows_two:
                return value.T
            high = value.astype(jnp.bfloat16).astype(jnp.float32)
            return jnp.concatenate([high, value - high], axis=0).T

        for start in range(0, block, 2):
            result = None
            for slot in range(slots):
                field = None
                first = 0
                for (members, _), table_ref in zip(groups, table_refs):
                    last = first + len(members)
                    value = jnp.concatenate(
                        [columns(slot, start + inner, first, last) for inner in range(2)],
                        axis=0,
                    )
                    if value.shape[1] * 3 == table_ref.shape[0]:
                        value = right_dot(value, table_ref[...])
                    else:
                        value = value.astype(jnp.bfloat16)
                        value = jnp.dot(
                            jnp.concatenate([value, value], axis=1),
                            jnp.concatenate(
                                [table_ref[...], jnp.zeros_like(table_ref[: value.shape[1] // 2])],
                                axis=0,
                            ),
                            preferred_element_type=jnp.float32,
                        )
                    field = value if field is None else field + value
                    first = last
                field = field.reshape(2, rows_two, length)
                term = field * factors_ref[slot, start : start + 2]
                result = term if result is None else result + term
            if total is not None:
                result = result + refs[-2][start : start + 2]
            out_ref[start : start + 2] = result

    space = pl.BlockSpec((block, rows_two, length), lambda i: (i, 0, 0))
    operands = [factors] + tables + parts
    in_specs = (
        [pl.BlockSpec((slots, block, rows_two, length), lambda i: (0, i, 0, 0))]
        + [pl.BlockSpec(table.shape, lambda i: (0, 0)) for table in tables]
        + [
            pl.BlockSpec(part.shape[:3] + (block, rows_two), lambda i: (0, 0, 0, i, 0))
            for part in parts
        ]
    )
    if total is not None:
        operands.append(total)
        in_specs.append(space)
    size = rows_one * rows_two
    planes_count = sum(part.shape[0] * part.shape[2] for part in parts)
    return pl.pallas_call(
        body,
        grid=(rows_one // block,),
        in_specs=in_specs,
        out_specs=space,
        out_shape=jax.ShapeDtypeStruct((rows_one, rows_two, length), jnp.float32),
        compiler_params=params(LAST_BYTES),
        cost_estimate=pl.CostEstimate(
            flops=6 * slots * size * planes_count * length,
            bytes_accessed=4 * size * (slots * planes_count + (2 + slots) * length),
            transcendentals=0,
        ),
        name="backward_last",
    )(*operands)


def cosine_turns():
    points = np.cos(np.pi * (np.arange(64) + 0.5) / 64) * 0.125 + 0.125
    fit = np.polynomial.Polynomial.fit(
        points, np.cos(2.0 * np.pi * np.sqrt(points)), 8, domain=[0.0, 0.25]
    )
    return [float(value) for value in fit.convert().coef]


def cosine_factors(saved, chosen, scale):
    rows_one, rows_two, length = saved.shape
    slots = chosen.shape[0]
    block = min(8, rows_one)
    coefficients = cosine_turns()

    def body(chosen_ref, saved_ref, out_ref):
        for slot in range(slots):
            feature = chosen_ref[slot]
            turns = saved_ref[...] * (feature * (1.0 / 16.0))
            turns = turns - jnp.round(turns)
            square = turns * turns
            result = jnp.full_like(square, coefficients[-1])
            for value in coefficients[-2::-1]:
                result = result * square + value
            out_ref[slot] = result * (feature * (math.pi / 8.0 * scale))

    size = rows_one * rows_two * length
    return pl.pallas_call(
        body,
        grid=(rows_one // block,),
        in_specs=[
            pl.BlockSpec(memory_space=pltpu.SMEM),
            pl.BlockSpec((block, rows_two, length), lambda i: (i, 0, 0)),
        ],
        out_specs=pl.BlockSpec((slots, block, rows_two, length), lambda i: (0, i, 0, 0)),
        out_shape=jax.ShapeDtypeStruct((slots, rows_one, rows_two, length), jnp.float32),
        compiler_params=params(),
        cost_estimate=pl.CostEstimate(
            flops=24 * slots * size, bytes_accessed=4 * size * (1 + slots), transcendentals=0
        ),
        name="cosine_factors",
    )(chosen, saved)


def swap_pairs(width_px, half_px, delta):
    return [(px, px // half_px * half_px + (px % half_px ^ delta)) for px in range(width_px)]


def send_messages(message, width_px):
    half_px = width_px // 2
    if half_px <= 8:
        return [message[0]] + [
            lax.ppermute(message[delta], "px", swap_pairs(width_px, half_px, delta))
            for delta in range(1, half_px)
        ]
    groups = [list(range(half_px)), list(range(half_px, width_px))]
    index = lax.axis_index("px") % half_px ^ jnp.arange(half_px)
    message = jnp.take(jnp.stack(message), index, axis=0)
    message = lax.all_to_all(message, "px", 0, 0, axis_index_groups=groups, tiled=True)
    message = jnp.take(message, index, axis=0)
    return [message[delta] for delta in range(half_px)]


def message_rows(spectra, edge, select, count):
    slots, length_one, local_two, length_three = spectra.shape
    half_one = length_one // 2
    half_px = half_one // local_two
    padded = select.shape[0] // half_px
    used = slots * (local_two + 3)
    extent = used + -used % 8
    group = 4
    lanes = 128

    def body(spectra_ref, edge_ref, select_ref, *refs):
        flats = [ref.reshape(count * extent, half_one) for ref in refs[:half_px]]
        scratch = refs[half_px:]

        def chosen(value):
            return lax.dot_general(
                select_ref[...],
                value.astype(jnp.bfloat16),
                (((1,), (1,)), ((), ())),
                preferred_element_type=jnp.float32,
            )

        def store(value, row):
            for delta in range(half_px):
                flats[delta][pl.ds(row, count, stride=extent), :] = value[
                    delta * padded : delta * padded + count
                ]

        for slot in range(slots):
            for part, ref in enumerate(scratch):
                ref[...] = (
                    spectra_ref[slot, :half_one, :, part * lanes : (part + 1) * lanes]
                    .astype(jnp.float32)
                    .reshape(half_one * local_two, lanes)
                )
            for start in range(0, local_two, group):
                value = jnp.concatenate(
                    [
                        jnp.concatenate(
                            [
                                ref[pl.ds(start + inner, half_one, stride=local_two), :]
                                for ref in scratch
                            ],
                            axis=1,
                        )
                        for inner in range(group)
                    ],
                    axis=0,
                )
                value = chosen(value)
                for inner in range(group):
                    store(
                        value[:, inner * half_one : (inner + 1) * half_one],
                        slot * local_two + start + inner,
                    )
            first = slots * local_two + 3 * slot
            store(chosen(edge_ref[slot, :half_one]), first)
            tiled = jnp.concatenate([spectra_ref[slot, half_one]] * half_px, axis=0)
            value = chosen(tiled)
            row = lax.broadcasted_iota(jnp.int32, value.shape, 0) // padded
            lane = lax.broadcasted_iota(jnp.int32, value.shape, 1) // local_two
            store(jnp.where(row == lane, value, 0.0), first + 1)
            corner = edge_ref[slot, half_one : half_one + 1]
            store(chosen(jnp.broadcast_to(corner, (half_one, length_three))), first + 2)
        for flat in flats:
            for row in range(used, extent):
                flat[pl.ds(row, count, stride=extent), :] = jnp.zeros(
                    (count, half_one), jnp.float32
                )

    part = (slots, half_one + 1, local_two, length_three)
    return pl.pallas_call(
        body,
        grid=(1,),
        in_specs=[
            pl.BlockSpec(part, lambda i: (0, 0, 0, 0)),
            pl.BlockSpec(edge.shape, lambda i: (0, 0, 0)),
            pl.BlockSpec(select.shape, lambda i: (0, 0)),
        ],
        out_specs=[pl.BlockSpec((count, extent, half_one), lambda i: (0, 0, 0))] * half_px,
        out_shape=[jax.ShapeDtypeStruct((count, extent, half_one), jnp.float32)] * half_px,
        scratch_shapes=[pltpu.VMEM((half_one * local_two, lanes), jnp.float32)]
        * (length_three // lanes),
        compiler_params=params(LAST_BYTES),
        cost_estimate=pl.CostEstimate(
            flops=2 * slots * select.shape[0] * half_one * local_two * length_three,
            bytes_accessed=2 * math.prod(part) + 4 * half_px * count * extent * half_one,
            transcendentals=0,
        ),
        name="message_rows",
    )(spectra, edge, select)


def kernel_messages(spectra, edge, wanted, width_px, width_py):
    slots, length_one, local_two, length_three = spectra.shape
    half_one = length_one // 2
    half_px = width_px // 2
    count = wanted.shape[1]
    px_index = lax.axis_index("px")
    py_index = lax.axis_index("py")
    wanted = wanted.reshape(width_px, width_py, count)
    sources = np.arange(width_px)
    targets = np.stack(
        [sources // half_px * half_px + (sources % half_px ^ d) for d in range(half_px)],
        axis=1,
    )
    rows = jnp.asarray(wanted[targets].transpose(0, 2, 1, 3).reshape(-1, half_px * count))
    rows = rows[px_index * width_py + py_index]
    sublanes = 16
    if local_two % sublanes == 0:
        padded = count + -count % sublanes
        rows = rows.reshape(half_px, count)
        rows = jnp.pad(rows, ((0, 0), (0, padded - count)), constant_values=-1)
        rows = rows.reshape(-1)
        select = (rows[:, None] == jnp.arange(length_three)[None, :]).astype(jnp.bfloat16)
        return message_rows(spectra, edge, select, count)
    select = (rows[:, None] == jnp.arange(length_three)[None, :]).astype(jnp.bfloat16)
    chosen = jnp.einsum(
        "rk,jabk->rjba",
        select,
        spectra[:, : half_one + 1],
        preferred_element_type=jnp.float32,
    )
    chosen_edge = jnp.einsum(
        "rk,jak->rja",
        select.astype(jnp.float32),
        edge,
        precision=lax.Precision.HIGHEST,
        preferred_element_type=jnp.float32,
    )
    body = chosen[..., :half_one].reshape(half_px, count, slots * local_two, half_one)
    edge_two = chosen_edge[..., None, :half_one]
    corner = jnp.broadcast_to(chosen_edge[..., None, half_one:], edge_two.shape)
    last = chosen[..., half_one].reshape(half_px, count, slots, local_two)
    edge_one = jnp.stack(
        [
            jnp.pad(
                last[delta],
                (
                    (0, 0),
                    (0, 0),
                    (delta * local_two, (half_px - 1 - delta) * local_two),
                ),
            )
            for delta in range(half_px)
        ]
    )
    edge_one = edge_one.reshape(half_px * count, slots, 1, half_px * local_two)
    edges = jnp.concatenate([edge_two, edge_one, corner], axis=2)
    edges = edges.reshape(half_px, count, 3 * slots, half_one)
    spare = -(slots * (local_two + 3)) % 8
    message = jnp.concatenate([body, edges], axis=2)
    message = jnp.pad(message, ((0, 0), (0, 0), (0, spare), (0, 0)))
    return [message[delta] for delta in range(half_px)]


def on_device(adjoint, saved, spectra, freq_index, picked):
    width_px = lax.axis_size("px")
    width_py = lax.axis_size("py")
    px_index = lax.axis_index("px")
    py_index = lax.axis_index("py")
    devices = width_px * width_py
    half_px = width_px // 2
    half_devices = devices // 2
    half_index = px_index // half_px
    px_low = px_index % half_px
    rows_one, rows_two, length_three = adjoint.shape
    length_one = rows_one * width_px
    length_two = rows_two * width_py
    slots = picked.shape[0]

    order = paired_order(length_three)
    shared_depth = 8
    shared_chunks = SHARED if length_three % (8 * devices * SHARED) == 0 else 0
    shared_count = half_devices * shared_depth
    shared = [
        order[chunk * shared_count : (chunk + 1) * shared_count].reshape(half_devices, -1)
        for chunk in range(shared_chunks)
    ]
    single = order[shared_chunks * shared_count :].reshape(devices, -1)
    depth = single.shape[1]
    owned = [np.concatenate([chunk, chunk]) for chunk in shared] + [single]

    def folded_rows(members):
        folded = np.concatenate(members, axis=1)
        folded = np.minimum(folded, length_three - folded)
        distinct = [list(dict.fromkeys(row.tolist())) for row in folded]
        count = max(len(row) for row in distinct)
        wanted = np.array([row + [row[-1]] * (count - len(row)) for row in distinct])
        places = [[row.index(k) for k in ks] for row, ks in zip(distinct, folded)]
        return wanted, np.array(places)

    half_one = length_one // 2
    edge = lax.ppermute(
        spectra[:, : half_one + 1, 0].astype(jnp.float32),
        "px",
        [(0, half_px), (half_px, 0)],
    )
    last = hartley(length_three)

    def send(value, runs):
        depth = sum(run.shape[1] for run in runs)
        table = left_table(last[np.concatenate([run.reshape(-1) for run in runs])])
        copies = []
        row = 0
        place = 0
        for run in runs:
            for owner in range(run.shape[0]):
                owners = range(owner, devices, run.shape[0])
                planes = [target * depth + place for target in owners]
                copies.append((row, run.shape[1], planes))
                row += run.shape[1]
            place += run.shape[1]
        return forward_last(value, table, devices * depth, copies).reshape(
            devices, depth, rows_one, rows_two
        )

    sent = send(adjoint, shared[:1] + [single])

    def exchange(value):
        return lax.all_to_all(value, ("px", "py"), 0, 0, tiled=True)

    def arranged(value):
        return value.reshape(width_px, width_py, -1, rows_one, rows_two)

    barrier = lax.optimization_barrier
    device = px_index * width_py + py_index
    sent, spectra, edge, adjoint = barrier((sent, spectra, edge, adjoint))
    wanted, places = folded_rows(owned)
    messages = kernel_messages(spectra, edge, wanted, width_px, width_py)
    messages, saved, adjoint, px_index, py_index = barrier(
        (messages, saved, adjoint, px_index, py_index)
    )
    half_index = px_index // half_px
    px_low = px_index % half_px
    messages = send_messages(messages, width_px)
    places = jnp.asarray(places, dtype=jnp.int32)[device]
    local_two = length_two // width_px
    special = (px_low * local_two).astype(jnp.int32).reshape(1)

    order_one = np.arange(length_one // 2)
    order_one = np.concatenate([order_one, (length_one - order_one) % length_one])
    order_one[length_one // 2] = length_one // 2
    slabs = half_index * half_px + (px_low ^ jnp.arange(half_px))
    order_two = (slabs[:, None] * local_two + jnp.arange(local_two)[None, :]).reshape(-1)
    order_two = jnp.concatenate([order_two, partners(order_two, length_two)])
    one = hartley(length_one)[order_one]
    one_f = left_table(one)
    one_b = left_table(one.T)
    sites_two = jnp.arange(length_two)
    two_f = traced_table(sites_two, order_two, length_two, 0)
    two_b = traced_table(order_two, sites_two, length_two, 0)
    sites_half = (slabs[:, None] * rows_one + jnp.arange(rows_one)[None, :]).reshape(-1)
    half_one_b = traced_table(sites_half, jnp.asarray(order_one), length_one, 1)
    near_two = (sites_two + py_index * rows_two) % length_two
    near_two_b = traced_table(order_two, near_two, length_two, 0)
    tables = (one_f, two_f, one_b, two_b)
    half_tables = (one_f, two_f, half_one_b, near_two_b)

    feature_ids = jnp.arange(freq_index.shape[0], dtype=jnp.int32)
    chosen = jnp.sum(
        jnp.where(feature_ids[None, :] == picked[:, None], freq_index[None, :], 0), axis=1
    ).astype(jnp.float32)

    shared_source = (
        (px_low ^ jnp.arange(half_px))[None, :] * width_py
        + ((py_index - jnp.arange(width_py)) % width_py)[:, None]
    ).reshape(-1)

    def shared_fields(index, value):
        first = index * shared_depth
        return filter_planes(
            arranged(value),
            0,
            messages,
            places[first : first + shared_depth],
            special,
            half_tables,
            slots,
            True,
        )

    def shared_rows(pieces):
        return [pieces[0]] + [
            lax.ppermute(pieces[delta], "px", swap_pairs(width_px, half_px, delta))
            for delta in range(1, half_px)
        ]

    def shared_group(index, pieces):
        parts = [jnp.stack([piece[0] for piece in pieces])]
        for shift in range(1, width_py):
            pairs = [(c, (c + shift) % width_py) for c in range(width_py)]
            far = jnp.stack([piece[shift] for piece in pieces])
            parts.append(lax.ppermute(far, "py", pairs))
        return parts, shared_tables[index]

    shared_tables = []
    for chunk in shared:
        ids = jnp.asarray(chunk)[shared_source].reshape(-1)
        shared_tables.append(
            traced_table(ids, jnp.arange(length_three), length_three, 0)
        )
    scale = 1.0 / (length_one * length_two * length_three)
    single_table = right_table(last[single.reshape(-1)])
    first = shared_chunks * shared_depth

    def single_fields(value):
        return filter_planes(
            arranged(value),
            min(first, shared_depth),
            messages,
            places[first:],
            special,
            tables,
            slots,
            False,
        ).reshape(devices, slots, depth, rows_one, rows_two)

    factors = cosine_factors(saved, chosen, scale)
    if shared_chunks == 0:
        returned = exchange(single_fields(exchange(sent)))
        return backward_last([([returned], single_table)], factors, None)

    arrived = exchange(sent)
    sent = send(adjoint, shared[1:])
    sent, messages, places, tables, half_tables, shared_tables, factors = barrier(
        (sent, messages, places, tables, half_tables, shared_tables, factors)
    )
    arrived_late = exchange(sent)
    near = shared_rows(shared_fields(0, arrived))
    fields_single = single_fields(arrived)
    fields_single, near = barrier((fields_single, near))
    returned = exchange(fields_single)
    pieces = shared_fields(1, arrived_late)
    pieces, near = barrier((pieces, near))
    group = shared_group(0, near)
    late = shared_rows(pieces)
    total = backward_last([group], factors, None)
    late, total = barrier((late, total))
    return backward_last(
        [shared_group(1, late), ([returned], single_table)], factors, total
    )


def solution(mesh):
    placed = (
        P(("chain", "px"), "py", None),
        P(("chain", "px"), "py", None),
        P(None, None, "px", None),
        P(),
        P(),
    )
    return jax.shard_map(
        on_device,
        mesh=mesh,
        in_specs=placed,
        out_specs=P(("chain", "px"), "py", None),
        check_vma=False,
    )
```
